32 devices in a mesh: dp: 8 (over z, x), mp: 4 (over y, core).
Axes of the slice: x: 2, y: 2, z: 4, core: 2. Of those that a mesh axis runs over, the one named last changes fastest.
Arguments:
- tokens: bfloat16 [16384, 896], P(('dp', 'mp')), may hold values from -6 to 6
- seq_lengths: int32 [8, 3], P('dp'), may hold values from 1 to 1536, as said below
- attn_gain: bfloat16 [896], replicated, may hold values from 0.5 to 1.5
- qkv_weight: bfloat16 [896, 1152], replicated, may hold values from -0.1875 to 0.1875
- qkv_bias: bfloat16 [1152], replicated, may hold values from -3 to 3
- out_weight: bfloat16 [896, 896], replicated, may hold values from -3.5 to 3.5
- mlp_gain: bfloat16 [896], replicated, may hold values from 0.5 to 1.5
- gate_weight: bfloat16 [896, 4864], P(None, 'mp'), may hold values from -0.1875 to 0.1875
- up_weight: bfloat16 [896, 4864], P(None, 'mp'), may hold values from -0.1875 to 0.1875
- down_weight: bfloat16 [4864, 896], P('mp'), may hold values from -0.078125 to 0.078125
- cotangent: bfloat16 [16384, 896], P(('dp', 'mp')), may hold values from -6 to 6
Outputs:
- output: bfloat16 [16384, 896], P(('dp', 'mp'))
- grad_tokens: float32 [16384, 896], P(('dp', 'mp'))
- grad_attn_gain: float32 [896], replicated
- grad_qkv_weight: float32 [896, 1152], replicated
- grad_qkv_bias: float32 [1152], replicated
- grad_out_weight: float32 [896, 896], replicated
- grad_mlp_gain: float32 [896], replicated
- grad_gate: float32 [896, 4864], P('dp', 'mp')
- grad_up: float32 [896, 4864], P('dp', 'mp')
- grad_down: float32 [4864, 896], P('mp', 'dp')
The draws below stay inside these ranges and needn't reach their ends.
Inputs may be any that keep to these rules, and one draw needn't show every extreme that they name: `seq_lengths`: each row sums to 2048; its middle entry is 1536; its first and last entries are positive and sum to 512; in some row the first entry is 1.
All inputs are finite; a program needn't handle non-finite values.
Results may differ from the reference program's by a relative error of at most 0.011.
Values may be sent and summed in bfloat16 or wider, within the bound.
No kernel may reach another device: no remote copies, remote signals or barrier semaphores. Data moves between devices by JAX's collectives and lax.ppermute only.
A program may use at most 256 MiB of HBM per device.

```python
import jax
import jax.numpy as jnp
from jax import lax

D = 896
FF = 4864
HEADS = 14
KV_HEADS = 2
HEAD = 64
TOK_DEV = 512
GROUP = 2048
TOKENS = 16384
QKV_COLS = 1152
N_DP = 8
N_MP = 4


def draw_seq_lengths(key, part):
    key = jax.random.fold_in(key, 11)
    length_key, pick_key = jax.random.split(key)
    group_rows = TOK_DEV * N_MP
    longest = group_rows - TOK_DEV
    first_part = jax.random.randint(length_key, (N_DP,), 1, TOK_DEV).astype(jnp.int32)
    chosen = jax.random.randint(pick_key, (), 0, N_DP).astype(jnp.int32)
    first_part = jnp.where(jnp.arange(N_DP, dtype=jnp.int32) == chosen, 1, first_part).astype(jnp.int32)
    last_part = (TOK_DEV - first_part).astype(jnp.int32)
    middle_part = jnp.full((N_DP,), longest, jnp.int32)
    return jnp.stack([first_part, middle_part, last_part], axis=1).astype(jnp.int32)


def level_of(rng, dims, shards, smallest, largest):
    factor_of = 1.0
    for dim, parts in shards:
        heights = jax.random.uniform(jax.random.fold_in(jax.random.fold_in(rng, 6), dim), (parts,), jnp.float32, smallest / len(shards), largest / len(shards))
        factor_of = factor_of * jnp.repeat(jnp.exp(heights), dims[dim] // parts).reshape((-1,) + (1,) * (len(dims) - 1 - dim))
    return factor_of


def noise(own_key, shape, spread, limit, cuts=(), kind=jnp.bfloat16):
    drawn = jax.random.normal(own_key, shape, jnp.float32) * spread
    if len(cuts) > 0:
        drawn = level_of(own_key, shape, cuts, -0.22, 0.18) * drawn
    return jnp.clip(drawn, min=-limit, max=limit).astype(kind)


def setup_inputs(seed: int = 0) -> dict:
    key_of = jax.random.split(jax.random.key(seed), 12)
    tokens = noise(key_of[0], (TOKENS, D), 1.0, 6.0, ((0, 32),))
    seq_lengths = draw_seq_lengths(jax.random.fold_in(key_of[11], 71), 0)
    attn_gain = jnp.clip(1.0 + 0.1 * jax.random.normal(key_of[2], (D,), jnp.float32), 0.5, 1.5).astype(jnp.bfloat16)
    qkv_weight = noise(key_of[3], (D, QKV_COLS), D ** -0.5, 0.1875)
    qkv_bias = noise(key_of[4], (QKV_COLS,), 0.5, 3.0)
    out_weight = noise(key_of[5], (HEADS * HEAD, D), (max(D // 256, 1)) ** -0.5, 3.5)
    mlp_gain = jnp.clip(1.0 + 0.1 * jax.random.normal(key_of[6], (D,), jnp.float32), 0.5, 1.5).astype(jnp.bfloat16)
    gate_weight = noise(key_of[7], (D, FF), D ** -0.5, 0.1875, ((1, 4),))
    up_weight = noise(key_of[8], (D, FF), D ** -0.5, 0.1875, ((1, 4),))
    down_weight = noise(key_of[9], (FF, D), FF ** -0.5, 0.078125, ((0, 4),))
    cotangent = noise(key_of[10], (TOKENS, D), 1.0, 6.0, ((0, 32),))
    return {"tokens": tokens, "seq_lengths": seq_lengths, "attn_gain": attn_gain, "qkv_weight": qkv_weight, "qkv_bias": qkv_bias, "out_weight": out_weight, "mlp_gain": mlp_gain, "gate_weight": gate_weight, "up_weight": up_weight, "down_weight": down_weight, "cotangent": cotangent}


norm_epsilon = 1e-06
rope_base = 1000000.0
masked_score = -1e+30
highest = lax.Precision.HIGHEST

@jax.custom_vjp
def low(v):
    return lax.optimization_barrier(v.astype(jnp.bfloat16)).astype(jnp.float32)

@jax.custom_vjp
def low_back(v):
    return v

def low_keep(v):
    return (low(v), None)

def low_pass(kept, grad):
    return (grad,)

def back_keep(v):
    return (v, None)

def back_low(kept, grad):
    return (low(grad),)
low.defvjp(low_keep, low_pass)
low_back.defvjp(back_keep, back_low)

def rope_tables(position, head_size):
    half_size = head_size // 2
    inverse_freq = rope_base ** (-2.0 * jnp.arange(half_size, dtype=jnp.float32) / head_size)
    angles = position.astype(jnp.float32)[:, None] * inverse_freq[None, :]
    return (jnp.cos(angles)[:, None, :], jnp.sin(angles)[:, None, :])

def rotate(values, cos_table, sin_table):
    half_size = values.shape[-1] // 2
    lower_half = values[..., :half_size]
    upper_half = values[..., half_size:]
    return jnp.concatenate([lower_half * cos_table - upper_half * sin_table, upper_half * cos_table + lower_half * sin_table], axis=-1)

def rms_scale(values, gain_vec):
    mean_sq = lax.optimization_barrier(jnp.mean(values * values, axis=-1, keepdims=True))
    return values * lax.rsqrt(mean_sq + norm_epsilon) * gain_vec

def layout(length_row, positions):
    seq_ends = jnp.cumsum(length_row)
    segment = lax.optimization_barrier(jnp.sum((positions[:, None] >= seq_ends[None, :]).astype(jnp.int32), axis=1))
    starts = seq_ends - length_row
    slot_ids = jnp.arange(length_row.shape[0], dtype=jnp.int32)
    seq_begin = lax.optimization_barrier(jnp.sum(jnp.where(segment[:, None] == slot_ids[None, :], starts[None, :], 0), axis=1))
    return (segment, positions - seq_begin)

def block_forward(inputs, attn_gain, qkv_weight, qkv_bias, out_weight, mlp_gain, gate_weight, up_weight, down_weight, segment, position):
    tok_rows = inputs.shape[0]
    q_width = HEADS * HEAD
    kv_width = KV_HEADS * HEAD
    normed = low(rms_scale(inputs, attn_gain))
    projected = jnp.dot(normed, qkv_weight, precision=highest) + qkv_bias
    cos_table, sin_table = rope_tables(position, HEAD)
    queries = low(rotate(low_back(projected[:, :q_width]).reshape(tok_rows, HEADS, HEAD), cos_table, sin_table))
    keys_all = low(rotate(low_back(projected[:, q_width:q_width + kv_width]).reshape(tok_rows, KV_HEADS, HEAD), cos_table, sin_table))
    values_all = low(low_back(projected[:, q_width + kv_width:])).reshape(tok_rows, KV_HEADS, HEAD)
    repeat_count = HEADS // KV_HEADS
    key_heads = jnp.repeat(keys_all.transpose(1, 0, 2), repeat_count, axis=0)
    value_heads = jnp.repeat(values_all.transpose(1, 0, 2), repeat_count, axis=0)
    query_heads = queries.transpose(1, 0, 2)
    allowed = (segment[:, None] == segment[None, :]) & (position[:, None] >= position[None, :])
    score_scale = HEAD ** (-0.5)

    def attend(head_parts):
        query_head, key_head, value_head = head_parts
        scores = low_back(jnp.dot(query_head, key_head.T, precision=highest) * score_scale)
        scores = jnp.where(allowed, scores, masked_score)
        row_max = lax.optimization_barrier(jnp.max(scores, axis=1, keepdims=True))
        weights = jnp.exp(scores - row_max)
        attn_prob = weights / lax.optimization_barrier(jnp.sum(weights, axis=1, keepdims=True))
        return jnp.dot(low(attn_prob), value_head, precision=highest)
    attended = lax.map(jax.checkpoint(attend), (query_heads, key_heads, value_heads))
    attended = low(low_back(attended.transpose(1, 0, 2).reshape(tok_rows, q_width)))
    middle = inputs + low_back(jnp.dot(attended, out_weight, precision=highest))
    normed_mid = low(rms_scale(middle, mlp_gain))
    gate_act = low_back(jnp.dot(normed_mid, gate_weight, precision=highest))
    up_act = low_back(jnp.dot(normed_mid, up_weight, precision=highest))
    hidden = low(jax.nn.silu(gate_act) * up_act)
    return middle + low_back(jnp.dot(hidden, down_weight, precision=highest))

def reference(tokens, seq_lengths, attn_gain, qkv_weight, qkv_bias, out_weight, mlp_gain, gate_weight, up_weight, down_weight, cotangent):
    params = tuple((weight.astype(jnp.float32) for weight in (attn_gain, qkv_weight, qkv_bias, out_weight, mlp_gain, gate_weight, up_weight, down_weight)))
    groups = tokens.astype(jnp.float32).reshape(N_DP, GROUP, D)
    cot_groups = cotangent.astype(jnp.float32).reshape(N_DP, GROUP, D)
    group_positions = jnp.arange(GROUP, dtype=jnp.int32)

    def group_step(summed, group_item):
        inputs, grad_output, length_row = group_item
        segment, position = layout(length_row, group_positions)

        def forward(inputs, *weights):
            return block_forward(inputs, *weights, segment, position)
        result, pullback = jax.vjp(forward, inputs, *params)
        group_grads = pullback(grad_output)
        summed = tuple((left_term + right_term for left_term, right_term in zip(summed, group_grads[1:])))
        return (summed, (result, group_grads[0]))
    zero_grads = tuple((jnp.zeros_like(weight) for weight in params))
    summed, (results, input_grads) = lax.scan(group_step, zero_grads, (groups, cot_groups, seq_lengths))
    output = results.reshape(TOKENS, D).astype(jnp.bfloat16)
    grad_tokens = input_grads.reshape(TOKENS, D)
    return (output, grad_tokens, summed[0], summed[1], summed[2], summed[3], summed[4], summed[5], summed[6], summed[7])
```

```python
import functools

import jax
import jax.numpy as jnp
from jax import lax
from jax.experimental import pallas as pl
from jax.experimental.pallas import tpu as pltpu
from jax.sharding import PartitionSpec as P

HEADS = 14
KV_HEADS = 2
HEAD = 64
MARKS = 16

norm_epsilon = 1e-06
rope_base = 1000000.0
masked_score = -1e30
vmem_bytes = 52 * 2**20


def dot(left, right, left_dim, right_dim):
    return lax.dot_general(
        left, right, (((left_dim,), (right_dim,)), ((), ())), preferred_element_type=jnp.float32
    )


def causal(tile):
    key_id = lax.broadcasted_iota(jnp.int32, tile.shape, 0)
    query_id = lax.broadcasted_iota(jnp.int32, tile.shape, 1)
    return jnp.where(key_id <= query_id, tile, masked_score)

def attend_kernel(bounds, q_ref, mark_ref, k_ref, v_ref, out_ref, log_ref, q_ext, acc, top):
    rows = q_ref.shape[1]
    half = rows // 2
    q_ext[0:HEAD, :] = q_ref[...]
    q_ext[HEAD:, :] = mark_ref[...]
    acc[...] = jnp.zeros_like(acc)
    top[...] = jnp.full_like(top, 2*masked_score)
    def tile(start, size, lo, hi, diag):
        keys = k_ref[0, pl.ds(start, size), :]
        scores = dot(keys, q_ext[:, lo:hi], 1, 0)
        if diag: scores = causal(scores)
        old = top[:, lo:hi]
        new = jnp.maximum(old, jnp.max(scores, axis=0, keepdims=True))
        weights = jnp.exp(scores - new).astype(jnp.bfloat16)
        top[:, lo:hi] = new
        acc[:, lo:hi] = acc[:, lo:hi]*jnp.exp(old-new) + dot(v_ref[0, :, pl.ds(start,size)], weights, 1, 0)
    first, own = bounds[0], bounds[1]
    def full(c, carry):
        tile(pl.multiple_of(c*rows, rows), rows, 0, rows, False)
        return carry
    lax.fori_loop(first, own, full, 0)
    base = pl.multiple_of(own*rows, rows)
    tile(base, half, half, rows, False)
    tile(base, half, 0, half, True)
    tile(pl.multiple_of(base+half, half), half, half, rows, True)
    total = acc[HEAD:HEAD+1, :]
    out_ref[...] = (acc[0:HEAD, :] / total).astype(jnp.bfloat16)
    log_ref[0] = top[...] + jnp.log(total)

def attend(bounds, q, marks_in, k, v):
    width, rows = q.shape
    heads = width // HEAD
    kv_heads, group, depth = k.shape
    rep = heads // kv_heads
    vd = v.shape[1]
    return pl.pallas_call(
        attend_kernel,
        grid_spec=pltpu.PrefetchScalarGridSpec(
            num_scalar_prefetch=1, grid=(heads,),
            in_specs=[
                pl.BlockSpec((HEAD, rows), lambda h, b: (h, 0)),
                pl.BlockSpec((MARKS, rows), lambda h, b: (0, 0)),
                pl.BlockSpec((1, group, depth), lambda h, b: (h // rep, 0, 0)),
                pl.BlockSpec((1, vd, group), lambda h, b: (h // rep, 0, 0)),
            ],
            out_specs=[
                pl.BlockSpec((HEAD, rows), lambda h, b: (h, 0)),
                pl.BlockSpec((1, 1, rows), lambda h, b: (h, 0, 0)),
            ],
            scratch_shapes=[pltpu.VMEM((depth, rows), jnp.bfloat16), pltpu.VMEM((vd, rows), jnp.float32), pltpu.VMEM((1, rows), jnp.float32)],
        ),
        out_shape=[jax.ShapeDtypeStruct((width, rows), jnp.bfloat16), jax.ShapeDtypeStruct((heads, 1, rows), jnp.float32)],
        compiler_params=pltpu.CompilerParams(vmem_limit_bytes=vmem_bytes),
        name="attend",
    )(bounds, q, marks_in, k, v)

def attend_back_kernel(bounds, q_ref, mark_ref, k_ref, kt_ref, vk_ref, o_ref, go_ref, log_ref, gq_ref, gk_ref, gv_ref, q_ext, acc, delta, *, rep):
    rows = q_ref.shape[1]
    half = rows // 2
    h = pl.program_id(0)
    q_ext[0:HEAD, :] = q_ref[...]
    q_ext[HEAD:, :] = mark_ref[...]
    acc[...] = jnp.zeros_like(acc)
    delta[...] = jnp.sum(o_ref[...].astype(jnp.float32)*go_ref[...].astype(jnp.float32), axis=0, keepdims=True)
    @pl.when(h % rep == 0)
    def _():
        gk_ref[...] = jnp.zeros_like(gk_ref)
        gv_ref[...] = jnp.zeros_like(gv_ref)
    def tile(start, size, lo, hi, diag):
        keys = k_ref[0, pl.ds(start, size), :]
        scores = dot(keys, q_ext[:, lo:hi], 1, 0)
        if diag: scores = causal(scores)
        prob = jnp.exp(scores - log_ref[0, :, lo:hi])
        go = go_ref[:, lo:hi]
        gprob = dot(vk_ref[0, pl.ds(start, size), :], go, 1, 0)
        gscore = (prob*(gprob - delta[:, lo:hi])).astype(jnp.bfloat16)
        prob = prob.astype(jnp.bfloat16)
        gv_ref[0, :, pl.ds(start, size)] += dot(go, prob, 1, 1)
        gk_ref[0, :, pl.ds(start, size)] += dot(q_ref[:, lo:hi], gscore, 1, 1)
        acc[:, lo:hi] += dot(kt_ref[0, :, pl.ds(start, size)], gscore, 1, 0)
    first, own = bounds[0], bounds[1]
    def full(c, carry):
        tile(pl.multiple_of(c*rows, rows), rows, 0, rows, False)
        return carry
    lax.fori_loop(first, own, full, 0)
    base = pl.multiple_of(own*rows, rows)
    tile(base, half, half, rows, False)
    tile(base, half, 0, half, True)
    tile(pl.multiple_of(base+half, half), half, half, rows, True)
    gq_ref[...] = acc[...]

def attend_back(bounds, q, marks_in, k, kt, vk, o, go, log):
    width, rows = q.shape
    heads = width // HEAD
    kv_heads, group, depth = k.shape
    rep = heads // kv_heads
    gshape = (kv_heads, HEAD, group)
    per_head = pl.BlockSpec((HEAD, rows), lambda h, b: (h, 0))
    def per_kv(shape): return pl.BlockSpec((1,)+tuple(shape[1:]), lambda h, b: (h // rep, 0, 0))
    return pl.pallas_call(
        functools.partial(attend_back_kernel, rep=rep),
        grid_spec=pltpu.PrefetchScalarGridSpec(
            num_scalar_prefetch=1, grid=(heads,),
            in_specs=[per_head, pl.BlockSpec((MARKS, rows), lambda h, b: (0, 0)), per_kv(k.shape), per_kv(kt.shape), per_kv(vk.shape), per_head, per_head, pl.BlockSpec((1, 1, rows), lambda h, b: (h, 0, 0))],
            out_specs=[per_head, per_kv(gshape), per_kv(gshape)],
            scratch_shapes=[pltpu.VMEM((depth, rows), jnp.bfloat16), pltpu.VMEM((HEAD, rows), jnp.float32), pltpu.VMEM((1, rows), jnp.float32)],
        ),
        out_shape=[jax.ShapeDtypeStruct((width, rows), jnp.float32), jax.ShapeDtypeStruct(gshape, jnp.float32), jax.ShapeDtypeStruct(gshape, jnp.float32)],
        compiler_params=pltpu.CompilerParams(vmem_limit_bytes=vmem_bytes),
        name="attend_back",
    )(bounds, q, marks_in, k, kt, vk, o, go, log)


def act_kernel(x_ref, cot_ref, gate_ref, up_ref, down_ref, out_ref, grad_ref, hid_ref, gg_ref, gu_ref):
    width = gate_ref.shape[1]
    step = 640 if width > 768 else width
    x = x_ref[...]
    cot = cot_ref[...]
    out = None
    for lo in range(0, width, step):
        cols = slice(lo, min(lo + step, width))
        gate = dot(x, gate_ref[:, cols], 1, 0)
        up = dot(x, up_ref[:, cols], 1, 0)
        grad_hidden = dot(cot, down_ref[cols, :], 1, 1)
        sig = jax.nn.sigmoid(gate)
        silu = gate * sig
        hidden = (silu * up).astype(jnp.bfloat16)
        grad_gate = (grad_hidden * up * (sig * (1.0 + gate * (1.0 - sig)))).astype(jnp.bfloat16)
        grad_up = (grad_hidden * silu).astype(jnp.bfloat16)
        hid_ref[:, cols] = hidden
        gg_ref[:, cols] = grad_gate
        gu_ref[:, cols] = grad_up
        part = dot(hidden, down_ref[cols, :], 1, 0)
        grad = dot(grad_gate, gate_ref[:, cols], 1, 1) + dot(grad_up, up_ref[:, cols], 1, 1)
        out = part if out is None else out + part
        total = grad if lo == 0 else total + grad
    out_ref[...] = out.astype(jnp.bfloat16)
    grad_ref[...] = total.astype(jnp.bfloat16)


def feed_forward(x, cot, gate_weight, up_weight, down_weight):
    rows, width = x.shape
    units = gate_weight.shape[1]
    tile = min(256, rows)
    by_rows = lambda cols: pl.BlockSpec((tile, cols), lambda i: (i, 0))
    whole = lambda w: pl.BlockSpec(w.shape, lambda i: (0, 0), pipeline_mode=pl.Buffered(1))
    shape = lambda cols: jax.ShapeDtypeStruct((rows, cols), jnp.bfloat16)
    return pl.pallas_call(
        act_kernel,
        grid=(rows // tile,),
        in_specs=[by_rows(width), by_rows(width), whole(gate_weight), whole(up_weight), whole(down_weight)],
        out_specs=[by_rows(width), by_rows(width), by_rows(units), by_rows(units), by_rows(units)],
        out_shape=[shape(width), shape(width), shape(units), shape(units), shape(units)],
        compiler_params=pltpu.CompilerParams(vmem_limit_bytes=vmem_bytes),
        cost_estimate=pl.CostEstimate(
            flops=12 * rows * width * units, bytes_accessed=6 * width * units + 6 * rows * units, transcendentals=rows * units
        ),
        name="feed_forward",
    )(x, cot, gate_weight, up_weight, down_weight)


def weight_kernel(*refs, groups, steps):
    out_ref, acc = refs[-2:]
    i = pl.program_id(0)

    @pl.when(i == 0)
    def _():
        acc[...] = jnp.zeros_like(acc)

    for g in range(groups):

        @pl.when(i // steps == g)
        def _():
            acc[...] += dot(refs[2 * g][...], refs[2 * g + 1][...], 0, 0)

    @pl.when(i == groups * steps - 1)
    def _():
        out_ref[...] = acc[...].astype(jnp.bfloat16)


def weight_grad(lefts, rights):
    rows, width = lefts[0].shape
    units = rights[0].shape[1]
    groups = len(lefts)
    tile = min(512, rows)
    steps = rows // tile
    args, specs = [], []
    for g in range(groups):
        place = lambda i, g=g: (jnp.clip(i - g * steps, 0, steps - 1), 0)
        args += [lefts[g], rights[g]]
        specs += [pl.BlockSpec((tile, width), place), pl.BlockSpec((tile, units), place)]
    return pl.pallas_call(
        functools.partial(weight_kernel, groups=groups, steps=steps),
        grid=(groups * steps,),
        in_specs=specs,
        out_specs=pl.BlockSpec((width, units), lambda i: (0, 0), pipeline_mode=pl.Buffered(1)),
        out_shape=jax.ShapeDtypeStruct((width, units), jnp.bfloat16),
        scratch_shapes=[pltpu.VMEM((width, units), jnp.float32)],
        compiler_params=pltpu.CompilerParams(vmem_limit_bytes=vmem_bytes),
        cost_estimate=pl.CostEstimate(
            flops=2 * groups * rows * width * units,
            bytes_accessed=2 * (groups * rows * (width + units) + width * units),
            transcendentals=0,
        ),
        name="weight_grad",
    )(*args)


def layout(length_row, positions):
    seq_ends = jnp.cumsum(length_row)
    segment = jnp.sum((positions[:, None] >= seq_ends[None, :]).astype(jnp.int32), axis=1)
    starts = seq_ends - length_row
    slot_ids = jnp.arange(length_row.shape[0], dtype=jnp.int32)
    seq_begin = jnp.sum(
        jnp.where(segment[:, None] == slot_ids[None, :], starts[None, :], 0), axis=1
    )
    return (segment, positions - seq_begin)


def rotate(values, cos_table, sin_table):
    rows = values.shape[1]
    halves = values.reshape(-1, 2, HEAD // 2, rows)
    lower, upper = halves[:, 0], halves[:, 1]
    turned = jnp.stack(
        [lower * cos_table - upper * sin_table, upper * cos_table + lower * sin_table], axis=1
    )
    return turned.reshape(-1, rows)


def rms_apply(values, gain_vec):
    inverse = lax.rsqrt(jnp.mean(values * values, axis=-1, keepdims=True) + norm_epsilon)
    return (values * inverse * gain_vec, inverse)


def rms_back(values, inverse, gain_vec, grad_out):
    scaled = grad_out * gain_vec
    mean_dot = jnp.mean(values * scaled, axis=-1, keepdims=True)
    grad_in = inverse * scaled - values * inverse * inverse * inverse * mean_dot
    grad_gain = jnp.sum(grad_out * values * inverse, axis=0)
    return (grad_in, grad_gain)


def after(value, earlier):
    return lax.optimization_barrier((value, earlier))[0]


def swap(value, axis, bit):
    count = lax.axis_size(axis)
    return lax.ppermute(value, axis, [(i, i ^ bit) for i in range(count)])


def high_bits(count):
    bits, bit = [], 2
    while bit < count:
        bits.append(bit)
        bit *= 2
    return bits


def spread_far(value):
    blocks = {0: value}
    for bit in high_bits(lax.axis_size("mp")):
        for offset in sorted(blocks):
            blocks[offset | bit] = swap(blocks[offset], "mp", bit)
    return blocks


def collect_near(parts):
    return {
        offset: parts[offset].astype(jnp.float32) + swap(parts[offset | 1], "mp", 1).astype(jnp.float32)
        for offset in parts
        if offset % 2 == 0
    }


def collect_far(parts):
    for bit in high_bits(lax.axis_size("mp")):
        parts = {
            offset: parts[offset] + swap(parts[offset | bit].astype(jnp.bfloat16), "mp", bit).astype(jnp.float32)
            for offset in parts
            if not offset & bit
        }
    return parts[0]


def halve(parts, axis, bit):
    mine = lax.rem(lax.axis_index(axis) // bit, 2)
    pairs = parts.reshape((parts.shape[0] // 2, 2) + parts.shape[1:])
    sent = lax.dynamic_index_in_dim(pairs, 1 - mine, 1, keepdims=False).astype(jnp.bfloat16)
    kept = lax.dynamic_index_in_dim(pairs, mine, 1, keepdims=False)
    return kept.astype(jnp.float32) + swap(sent, axis, bit).astype(jnp.float32)


def double(parts, axis, bit):
    mine = lax.rem(lax.axis_index(axis) // bit, 2)
    other = swap(parts, axis, bit)
    pairs = jnp.stack([jnp.where(mine == 0, parts, other), jnp.where(mine == 0, other, parts)], axis=1)
    return pairs.reshape((-1,) + parts.shape[1:])


def all_bits(count):
    return [1] + high_bits(count) if count > 1 else []


def scatter_dp(value):
    count = lax.axis_size("dp")
    parts = value.reshape(count, value.shape[0] // count, value.shape[1])
    for bit in all_bits(count):
        parts = halve(parts, "dp", bit)
    return parts[0]


def sum_everywhere(value):
    dp_count, mp_count = lax.axis_size("dp"), lax.axis_size("mp")
    rows, cols = value.shape
    share = -(-rows // (dp_count * mp_count))
    padded = jnp.pad(value, ((0, share * dp_count * mp_count - rows), (0, 0)))
    parts = padded.reshape(mp_count, dp_count * share, cols)
    for bit in all_bits(mp_count):
        parts = halve(parts, "mp", bit)
    pieces = parts.astype(jnp.bfloat16).reshape(dp_count, share, cols)
    for bit in all_bits(dp_count):
        pieces = halve(pieces, "dp", bit)
    pieces = pieces.astype(jnp.bfloat16)
    for bit in reversed(all_bits(dp_count)):
        pieces = double(pieces, "dp", bit)
    parts = pieces.reshape(1, dp_count * share, cols)
    for bit in reversed(all_bits(mp_count)):
        parts = double(parts, "mp", bit)
    return parts.reshape(-1, cols)[:rows].astype(jnp.float32)


def on_device(
    tokens,
    seq_lengths,
    attn_gain,
    qkv_weight,
    qkv_bias,
    out_weight,
    mlp_gain,
    gate_weight,
    up_weight,
    down_weight,
    cotangent,
):
    tok_rows, width = tokens.shape
    mp_count = lax.axis_size("mp")
    mp_index = lax.axis_index("mp")
    group_rows = tok_rows * mp_count
    q_width = HEADS * HEAD
    kv_width = KV_HEADS * HEAD
    score_scale = HEAD ** (-0.5)
    row_base = mp_index * tok_rows
    lengths = seq_lengths[0]
    own_rows = row_base + jnp.arange(tok_rows, dtype=jnp.int32)
    segment, position = layout(lengths, own_rows)
    key_segment, _ = layout(lengths, jnp.arange(group_rows, dtype=jnp.int32))
    bounds = jnp.stack([(row_base - position[0]) // tok_rows, mp_index]).astype(jnp.int32)
    marks = jnp.arange(MARKS, dtype=jnp.int32)
    query_marks = (segment[None, :] != marks[:, None]).astype(jnp.bfloat16)
    key_marks = jnp.where(key_segment[:, None] == marks[None, :], masked_score, 0.0).astype(jnp.bfloat16)
    inverse_freq = rope_base ** (-2.0 * jnp.arange(HEAD // 2, dtype=jnp.float32) / HEAD)
    angles = inverse_freq[:, None] * position.astype(jnp.float32)[None, :]
    cos_table, sin_table = jnp.cos(angles), jnp.sin(angles)

    inputs = tokens.astype(jnp.float32)
    attn_scale = attn_gain.astype(jnp.float32)
    normed_full, inverse_one = rms_apply(inputs, attn_scale)
    normed = normed_full.astype(jnp.bfloat16)
    projected = dot(qkv_weight, normed, 0, 1) + qkv_bias.astype(jnp.float32)[:, None]
    queries = rotate(projected[:q_width], cos_table, sin_table).astype(jnp.bfloat16) * jnp.bfloat16(score_scale)
    keys_own = rotate(projected[q_width : q_width + kv_width], cos_table, sin_table)
    own_kv = jnp.concatenate([keys_own, projected[q_width + kv_width :]], axis=0).astype(jnp.bfloat16)

    far = spread_far(own_kv)
    offsets = sorted(far)
    near = swap(jnp.stack([far[o] for o in offsets]), "mp", 1)
    blocks = {}
    for i, o in enumerate(offsets):
        blocks[o], blocks[o | 1] = far[o], near[i]
    for bit in all_bits(mp_count):
        mine = lax.rem(mp_index // bit, 2) == 0
        for o in range(mp_count):
            if not o & bit:
                low, high = blocks[o], blocks[o | bit]
                blocks[o], blocks[o | bit] = jnp.where(mine, low, high), jnp.where(mine, high, low)
    group_kv = jnp.concatenate([blocks[o] for o in range(mp_count)], axis=1)
    keys_t = group_kv[:kv_width].reshape(KV_HEADS, HEAD, group_rows)
    values_t = group_kv[kv_width:].reshape(KV_HEADS, HEAD, group_rows)
    keys = keys_t.transpose(0, 2, 1)
    values = values_t.transpose(0, 2, 1)
    marked_keys = jnp.concatenate([keys, jnp.broadcast_to(key_marks, (KV_HEADS,) + key_marks.shape)], axis=2)
    marked_values = jnp.concatenate([values_t, jnp.ones((KV_HEADS, MARKS, group_rows), jnp.bfloat16)], axis=1)

    cot_far = spread_far(after(cotangent, group_kv))
    cot_near = {o | 1: swap(cot_far[o], "mp", 1) for o in cot_far}
    cots = {**cot_far, **cot_near}

    attended, log_totals = attend(bounds, queries, query_marks, marked_keys, marked_values)
    middle = inputs + dot(attended, out_weight, 0, 0)
    mlp_scale = mlp_gain.astype(jnp.float32)
    normed_mid_full, inverse_two = rms_apply(middle, mlp_scale)
    normed_mid = normed_mid_full.astype(jnp.bfloat16)

    mids = spread_far(normed_mid)
    mids.update({o | 1: swap(mids[o], "mp", 1) for o in sorted(mids)})
    xs, cs, hids, ggs, gus = [], [], [], [], []
    outs, grads = {}, {}
    for o in range(0, mp_count, 2):
        x = jnp.concatenate([mids[o], mids[o | 1]], axis=0)
        c = jnp.concatenate([cots[o], cots[o | 1]], axis=0)
        out, grad, hid, gg, gu = feed_forward(x, c, gate_weight, up_weight, down_weight)
        xs.append(x), cs.append(c), hids.append(hid), ggs.append(gg), gus.append(gu)
        for k in (0, 1):
            outs[o | k] = out[k * tok_rows : (k + 1) * tok_rows]
            grads[o | k] = grad[k * tok_rows : (k + 1) * tok_rows]
    grad_normed_mid = collect_far(collect_near(grads))
    wide_gate = weight_grad(xs, ggs)
    wide_up = weight_grad(xs, gus)
    wide_down = weight_grad(cs, hids)
    grad_gate = scatter_dp(wide_gate)
    grad_up = scatter_dp(wide_up)
    grad_down = scatter_dp(wide_down).T
    mlp_out = collect_far(collect_near(after(outs, grad_normed_mid)))
    output = (middle + mlp_out).astype(jnp.bfloat16)

    grad_from_mid, grad_mlp_gain = rms_back(middle, inverse_two, mlp_scale, grad_normed_mid)
    grad_middle = cotangent.astype(jnp.float32) + grad_from_mid
    grad_branch = grad_middle.astype(jnp.bfloat16)
    grad_attended = dot(out_weight, grad_branch, 1, 1).astype(jnp.bfloat16)
    grad_queries, grad_keys, grad_values = attend_back(
        bounds, queries, query_marks, marked_keys, keys_t, values, attended, grad_attended, log_totals
    )
    grad_out_weight = sum_everywhere(dot(attended, grad_branch, 1, 0))

    grad_kv = jnp.concatenate([grad_keys.reshape(kv_width, group_rows), grad_values.reshape(kv_width, group_rows)], axis=0)
    kv_parts = {
        o: lax.dynamic_slice_in_dim(grad_kv, (mp_index ^ o) * tok_rows, tok_rows, 1).astype(jnp.bfloat16)
        for o in range(mp_count)
    }
    own_grad_kv = collect_far(collect_near(kv_parts))
    back_q = rotate(grad_queries * score_scale, cos_table, -sin_table)
    back_k = rotate(own_grad_kv[:kv_width], cos_table, -sin_table)
    grad_projected = jnp.concatenate([back_q, back_k, own_grad_kv[kv_width:]], axis=0).astype(jnp.bfloat16)
    grad_normed = dot(grad_projected, qkv_weight, 0, 1)
    grad_qkv = dot(normed, grad_projected, 0, 1)
    grad_bias = jnp.sum(grad_projected.astype(jnp.float32), axis=1)
    grad_from_first, grad_attn_gain = rms_back(inputs, inverse_one, attn_scale, grad_normed)
    grad_tokens = grad_middle + grad_from_first

    bias_cols = -(-grad_bias.shape[0] // width)
    bias_block = jnp.pad(grad_bias, (0, bias_cols * width - grad_bias.shape[0])).reshape(bias_cols, width)
    extra = jnp.concatenate([grad_attn_gain[None], grad_mlp_gain[None], bias_block], axis=0)
    extra = jnp.pad(extra, ((0, 128 - extra.shape[0]), (0, 0))).T
    summed = sum_everywhere(jnp.concatenate([grad_qkv, extra], axis=1))
    qkv_cols = grad_qkv.shape[1]
    sums = summed[:, qkv_cols : qkv_cols + 2 + bias_cols].T
    return (
        output,
        grad_tokens,
        sums[0],
        summed[:, :qkv_cols],
        sums[2:].reshape(-1)[: grad_bias.shape[0]],
        grad_out_weight,
        sums[1],
        grad_gate,
        grad_up,
        grad_down,
    )


def solution(mesh):
    return jax.shard_map(
        on_device,
        mesh=mesh,
        in_specs=(
            P(("dp", "mp"), None),
            P("dp", None),
            P(),
            P(),
            P(),
            P(),
            P(),
            P(None, "mp"),
            P(None, "mp"),
            P("mp", None),
            P(("dp", "mp"), None),
        ),
        out_specs=(
            P(("dp", "mp"), None),
            P(("dp", "mp"), None),
            P(),
            P(),
            P(),
            P(),
            P(),
            P("dp", "mp"),
            P("dp", "mp"),
            P("mp", "dp"),
        ),
        check_vma=False,
    )
```

```python
import functools

import jax
import jax.numpy as jnp
from jax import lax
from jax.experimental import pallas as pl
from jax.experimental.pallas import tpu as pltpu
from jax.sharding import PartitionSpec as P

HEADS = 14
KV_HEADS = 2
HEAD = 64
MARKS = 16

norm_epsilon = 1e-06
rope_base = 1000000.0
masked_score = -1e30
vmem_bytes = 52 * 2**20


anywhere = pl.BlockSpec(memory_space=pltpu.HBM)
light = pl.CostEstimate(flops=1000, bytes_accessed=1000, transcendentals=0)


def dot(left, right, left_dim, right_dim):
    return lax.dot_general(
        left, right, (((left_dim,), (right_dim,)), ((), ())), preferred_element_type=jnp.float32
    )


def causal(tile):
    key_id = lax.broadcasted_iota(jnp.int32, tile.shape, 0)
    query_id = lax.broadcasted_iota(jnp.int32, tile.shape, 1)
    return jnp.where(key_id <= query_id, tile, masked_score)


def turn(values, cos_table, sin_table):
    half = HEAD // 2
    pieces = []
    for row in range(0, values.shape[0], HEAD):
        lower, upper = values[row : row + half], values[row + half : row + HEAD]
        pieces += [lower * cos_table - upper * sin_table, upper * cos_table + lower * sin_table]
    return pieces


def project_kernel(tok_ref, gain_ref, weight_ref, bias_ref, cos_ref, sin_ref, normed_ref, q_ref, kv_ref):
    values = tok_ref[...].astype(jnp.float32)
    inverse = lax.rsqrt(jnp.mean(values * values, axis=-1, keepdims=True) + norm_epsilon)
    normed = (values * inverse * gain_ref[...].astype(jnp.float32)).astype(jnp.bfloat16)
    rows, width = normed.shape
    normed_ref[:, 0:width] = normed
    ones_at = lax.broadcasted_iota(jnp.int32, (rows, normed_ref.shape[1] - width), 1) == 0
    normed_ref[:, width:] = jnp.where(ones_at, 1.0, 0.0).astype(jnp.bfloat16)
    cos_table, sin_table = cos_ref[:, 0:rows], sin_ref[:, 0:rows]
    q_width, kv_width, half = HEADS * HEAD, KV_HEADS * HEAD, HEAD // 2
    step = 128
    for lo in range(0, weight_ref.shape[1], step):
        cols = slice(lo, lo + step)
        part = dot(normed, weight_ref[:, cols], 1, 0) + bias_ref[:, cols].astype(jnp.float32)
        part = part.T
        if lo < q_width + kv_width:
            pieces = turn(part, cos_table, sin_table)
        else:
            pieces = [part[r : r + half] for r in range(0, step, half)]
        for n, piece in enumerate(pieces):
            row = lo + n * half
            piece = piece.astype(jnp.bfloat16)
            if row < q_width:
                q_ref[row : row + half, :] = piece * jnp.bfloat16(HEAD ** (-0.5))
            else:
                row -= q_width
                which, row = row // kv_width, row % kv_width
                head, row = row // HEAD, row % HEAD
                place = (2 * head + which) * HEAD + row
                kv_ref[place : place + half, :] = piece


def project(tokens, gain, weight, bias, cos_table, sin_table):
    rows, width = tokens.shape
    shape = lambda *s: jax.ShapeDtypeStruct(s, jnp.bfloat16)
    return pl.pallas_call(
        project_kernel,
        out_shape=[shape(rows, width + 128), shape(HEADS * HEAD, rows), shape(2 * KV_HEADS * HEAD, rows)],
        compiler_params=pltpu.CompilerParams(vmem_limit_bytes=vmem_bytes),
        cost_estimate=light,
        name="project",
    )(tokens, gain[None], weight, bias[None], cos_table, sin_table)


def load_keys(blocks, marks_ref, kx, vx, vk):
    rows = blocks[0].shape[1]
    for o, block in enumerate(blocks):
        spot = slice(o * rows, (o + 1) * rows)
        flat = block[...].astype(jnp.float32).T.astype(jnp.bfloat16)
        kx[spot, 0:HEAD] = flat[:, 0:HEAD]
        if vk is not None:
            vk[spot, :] = flat[:, HEAD:]
        if vx is not None:
            vx[0:HEAD, spot] = block[HEAD:, :]
    kx[:, HEAD:] = marks_ref[...]
    if vx is not None:
        vx[HEAD:, :] = jnp.ones((MARKS, vx.shape[1]), jnp.bfloat16)


def staged(items, begin, finish):
    earlier = None
    for item in items:
        state = begin(item)
        if earlier is not None:
            finish(*earlier)
        earlier = (item, state)
    finish(*earlier)


def attend_kernel(bounds, q_ref, mark_ref, marks_ref, *refs, count):
    blocks = refs[:count]
    out_ref, log_ref, kx, vx, q_ext, acc, top = refs[-7:]
    rows = q_ref.shape[1]
    half = rows // 2
    heads = q_ref.shape[0] // HEAD
    load_keys(blocks, marks_ref, kx, vx, None)
    for h in range(heads):
        q_ext[h, 0:HEAD, :] = q_ref[h * HEAD : (h + 1) * HEAD, :]
        q_ext[h, HEAD:, :] = mark_ref[...]
    acc[...] = jnp.zeros_like(acc)
    top[...] = jnp.full_like(top, 2 * masked_score)

    def begin(item):
        h, start, size, lo, hi, diag = item
        scores = dot(kx[pl.ds(start, size), :], q_ext[h, :, lo:hi], 1, 0)
        return causal(scores) if diag else scores

    def finish(item, scores):
        h, start, size, lo, hi, diag = item
        old = top[h, :, lo:hi]
        new = jnp.maximum(old, jnp.max(scores, axis=0, keepdims=True))
        weights = jnp.exp(scores - new).astype(jnp.bfloat16)
        top[h, :, lo:hi] = new
        acc[h, :, lo:hi] = acc[h, :, lo:hi] * jnp.exp(old - new) + dot(vx[:, pl.ds(start, size)], weights, 1, 0)

    first, own = bounds[0], bounds[1]

    def whole(c, carry):
        start = pl.multiple_of((c ^ own) * rows, rows)
        staged([(h, start, rows, 0, rows, False) for h in range(heads)], begin, finish)
        return carry

    lax.fori_loop(first, own, whole, 0)
    spots = [(0, half, half, rows, False), (0, half, 0, half, True), (half, half, half, rows, True)]
    staged([(h,) + spot for h in range(heads) for spot in spots], begin, finish)
    for h in range(heads):
        total = acc[h, HEAD : HEAD + 1, :]
        out_ref[h * HEAD : (h + 1) * HEAD, :] = (acc[h, 0:HEAD, :] / total).astype(jnp.bfloat16)
        log_ref[h] = top[h] + jnp.log(total)


def attend(bounds, q, query_marks, key_marks, blocks, earlier):
    width, rows = q.shape
    heads = width // HEAD
    rep = heads // KV_HEADS
    group = key_marks.shape[0]
    whole = lambda a: pl.BlockSpec(a.shape, lambda g, b: (0, 0))
    by_head = lambda n: pl.BlockSpec((n, rows), lambda g, b: (g, 0))
    return pl.pallas_call(
        functools.partial(attend_kernel, count=len(blocks)),
        grid_spec=pltpu.PrefetchScalarGridSpec(
            num_scalar_prefetch=1,
            grid=(KV_HEADS,),
            in_specs=[by_head(rep * HEAD), whole(query_marks), whole(key_marks)] + [by_head(2 * HEAD)] * len(blocks) + [anywhere],
            out_specs=[by_head(rep * HEAD), pl.BlockSpec((rep, 1, rows), lambda g, b: (g, 0, 0))],
            scratch_shapes=[
                pltpu.VMEM((group, HEAD + MARKS), jnp.bfloat16),
                pltpu.VMEM((HEAD + MARKS, group), jnp.bfloat16),
                pltpu.VMEM((rep, HEAD + MARKS, rows), jnp.bfloat16),
                pltpu.VMEM((rep, HEAD + MARKS, rows), jnp.float32),
                pltpu.VMEM((rep, 1, rows), jnp.float32),
            ],
        ),
        out_shape=[
            jax.ShapeDtypeStruct((width, rows), jnp.bfloat16),
            jax.ShapeDtypeStruct((heads, 1, rows), jnp.float32),
        ],
        compiler_params=pltpu.CompilerParams(vmem_limit_bytes=vmem_bytes),
        cost_estimate=light,
        name="attend",
    )(bounds, q, query_marks, key_marks, *blocks, earlier)


def attend_back_kernel(
    bounds, q_ref, mark_ref, marks_ref, o_ref, go_ref, log_ref, cos_ref, sin_ref, *refs, count
):
    blocks = refs[:count]
    refs = refs[count + 1 :]
    gq_ref = refs[0]
    gkv_refs = refs[1:3]
    kx, vk, q_ext, acc, delta, gkv = refs[3:]
    rows = q_ref.shape[1]
    half = rows // 2
    heads = q_ref.shape[0] // HEAD
    load_keys(blocks, marks_ref, kx, None, vk)
    for h in range(heads):
        spot = slice(h * HEAD, (h + 1) * HEAD)
        q_ext[h, 0:HEAD, :] = q_ref[spot, :]
        q_ext[h, HEAD:, :] = mark_ref[...]
        product = o_ref[spot, :].astype(jnp.float32) * go_ref[spot, :].astype(jnp.float32)
        delta[h] = jnp.sum(product, axis=0, keepdims=True)
    acc[...] = jnp.zeros_like(acc)
    gkv[...] = jnp.zeros_like(gkv)

    def begin(item):
        h, start, size, lo, hi, diag, keys_t = item
        scores = dot(kx[pl.ds(start, size), :], q_ext[h, :, lo:hi], 1, 0)
        grad_prob = dot(vk[pl.ds(start, size), :], go_ref[h * HEAD : (h + 1) * HEAD, lo:hi], 1, 0)
        return (causal(scores) if diag else scores), grad_prob

    def finish(item, state):
        h, start, size, lo, hi, diag, keys_t = item
        scores, grad_prob = state
        spot = slice(h * HEAD, (h + 1) * HEAD)
        prob = jnp.exp(scores - log_ref[h, :, lo:hi])
        grad_score = (prob * (grad_prob - delta[h, :, lo:hi])).astype(jnp.bfloat16)
        gkv[HEAD:, pl.ds(start, size)] += dot(go_ref[spot, lo:hi], prob.astype(jnp.bfloat16), 1, 1)
        gkv[0:HEAD, pl.ds(start, size)] += dot(q_ref[spot, lo:hi], grad_score, 1, 1)
        acc[h, :, lo:hi] += dot(keys_t, grad_score, 1, 0)

    first, own = bounds[0], bounds[1]
    for o in range(1, count):
        c = own ^ o

        @pl.when((c >= first) & (c < own))
        def _():
            keys_t = blocks[o][0:HEAD, :]
            staged([(h, o * rows, rows, 0, rows, False, keys_t) for h in range(heads)], begin, finish)

    low, high = blocks[0][0:HEAD, 0:half], blocks[0][0:HEAD, half:]
    spots = [(0, half, half, rows, False, low), (0, half, 0, half, True, low), (half, half, half, rows, True, high)]
    staged([(h,) + spot for h in range(heads) for spot in spots], begin, finish)
    cos_own, sin_own = cos_ref[:, 0:rows], -sin_ref[:, 0:rows]
    for h in range(heads):
        pieces = turn(acc[h] * (HEAD ** (-0.5)), cos_own, sin_own)
        for n, piece in enumerate(pieces):
            row = h * HEAD + n * (HEAD // 2)
            gq_ref[row : row + HEAD // 2, :] = piece.astype(jnp.bfloat16)
    for o in range(count):
        spot = slice(o * rows, (o + 1) * rows)
        pieces = turn(gkv[0:HEAD, spot], cos_ref[:, spot], -sin_ref[:, spot])
        for n, piece in enumerate(pieces):
            gkv_refs[o % 2][o // 2, n * (HEAD // 2) : (n + 1) * (HEAD // 2), :] = piece.astype(jnp.bfloat16)
        gkv_refs[o % 2][o // 2, HEAD:, :] = gkv[HEAD:, spot].astype(jnp.bfloat16)


def attend_back(head, bounds, q, query_marks, key_marks, o, go, log, cos_table, sin_table, blocks, earlier):
    width, rows = q.shape
    rep = HEADS // KV_HEADS
    group = key_marks.shape[0]
    count = len(blocks)
    whole = lambda a: pl.BlockSpec(a.shape, lambda i, b: (0, 0))
    by_head = lambda n: pl.BlockSpec((n, rows), lambda i, b: (head, 0))
    return pl.pallas_call(
        functools.partial(attend_back_kernel, count=count),
        grid_spec=pltpu.PrefetchScalarGridSpec(
            num_scalar_prefetch=1,
            grid=(1,),
            in_specs=[by_head(rep * HEAD), whole(query_marks), whole(key_marks), by_head(rep * HEAD), by_head(rep * HEAD)]
            + [pl.BlockSpec((rep, 1, rows), lambda i, b: (head, 0, 0)), whole(cos_table), whole(sin_table)]
            + [by_head(2 * HEAD)] * count
            + [anywhere],
            out_specs=[pl.BlockSpec((rep * HEAD, rows), lambda i, b: (0, 0))]
            + [pl.BlockSpec((count // 2, 2 * HEAD, rows), lambda i, b: (0, 0, 0))] * 2,
            scratch_shapes=[
                pltpu.VMEM((group, HEAD + MARKS), jnp.bfloat16),
                pltpu.VMEM((group, HEAD), jnp.bfloat16),
                pltpu.VMEM((rep, HEAD + MARKS, rows), jnp.bfloat16),
                pltpu.VMEM((rep, HEAD, rows), jnp.float32),
                pltpu.VMEM((rep, 1, rows), jnp.float32),
                pltpu.VMEM((2 * HEAD, group), jnp.float32),
            ],
        ),
        out_shape=[jax.ShapeDtypeStruct((rep * HEAD, rows), jnp.bfloat16)]
        + [jax.ShapeDtypeStruct((count // 2, 2 * HEAD, rows), jnp.bfloat16)] * 2,
        compiler_params=pltpu.CompilerParams(vmem_limit_bytes=vmem_bytes),
        cost_estimate=light,
        name="attend_back",
    )(bounds, q, query_marks, key_marks, o, go, log, cos_table, sin_table, *blocks, earlier)


def act_kernel(*refs, count, steps):
    xs, cots = refs[:count], refs[count : 2 * count]
    gate_ref, up_ref, down_ref = refs[2 * count : 2 * count + 3]
    refs = refs[2 * count + 4 :]
    outs, grads = refs[:count], refs[count : 2 * count]
    hid_ref, gg_ref, gu_ref = refs[2 * count :]
    i = pl.program_id(0)

    def run(n):
        x = xs[n][...]
        gate = dot(x, gate_ref[...], 1, 1)
        up = dot(x, up_ref[...], 1, 1)
        grad_hidden = dot(cots[n][...], down_ref[...], 1, 1)
        sig = jax.nn.sigmoid(gate)
        silu = gate * sig
        hidden = (silu * up).astype(jnp.bfloat16)
        grad_gate = (grad_hidden * up * (sig * (1.0 + gate * (1.0 - sig)))).astype(jnp.bfloat16)
        grad_up = (grad_hidden * silu).astype(jnp.bfloat16)
        hid_ref[...] = hidden
        gg_ref[...] = grad_gate
        gu_ref[...] = grad_up
        grads[n][...] = (dot(grad_gate, gate_ref[...], 1, 0) + dot(grad_up, up_ref[...], 1, 0)).astype(jnp.bfloat16)
        outs[n][...] = dot(hidden, down_ref[...], 1, 0).astype(jnp.bfloat16)

    for n in range(count):
        pl.when(i // steps == n)(functools.partial(run, n))


def feed_forward(xs, cots, gate_t, up_t, down_weight, earlier):
    rows, width = xs[0].shape
    units = gate_t.shape[0]
    count = len(xs)
    tile = min(256, rows)
    steps = rows // tile

    def chunk(n):
        return pl.BlockSpec((tile, width), lambda i: (jnp.clip(i - n * steps, 0, steps - 1), 0))

    whole = lambda w: pl.BlockSpec(w.shape, lambda i: (0, 0), pipeline_mode=pl.Buffered(1))
    by_rows = pl.BlockSpec((tile, units), lambda i: (i, 0))
    small = jax.ShapeDtypeStruct((rows, width), jnp.bfloat16)
    large = jax.ShapeDtypeStruct((count * rows, units), jnp.bfloat16)
    result = pl.pallas_call(
        functools.partial(act_kernel, count=count, steps=steps),
        grid=(count * steps,),
        in_specs=[chunk(n) for n in range(count)] * 2 + [whole(gate_t), whole(up_t), whole(down_weight), anywhere],
        out_specs=[chunk(n) for n in range(count)] * 2 + [by_rows] * 3,
        out_shape=[small] * (2 * count) + [large] * 3,
        compiler_params=pltpu.CompilerParams(vmem_limit_bytes=vmem_bytes),
        cost_estimate=light,
        name="feed_forward",
    )(*xs, *cots, gate_t, up_t, down_weight, earlier)
    return result[:count], result[count : 2 * count], *result[2 * count :]


def weight_kernel(place, *refs, count, groups, bit):
    lefts, rights = refs[:count], refs[count : count + groups]
    sent_ref, kept_ref, acc = refs[-3:]
    i = pl.program_id(0)

    for n in range(count):

        @pl.when(i == n)
        def _():
            product = dot(lefts[n][...], rights[n * groups // count][...], 0, 0)
            acc[...] = product if n == 0 else acc[...] + product

    @pl.when(i == count - 1)
    def _():
        pieces, rows, _ = sent_ref.shape
        for ref, which in ((sent_ref, 1 - place[0]), (kept_ref, place[0])):
            for n in range(pieces):
                low, high = n % bit, n // bit
                start = (high * 2 * bit + low) * rows
                if rows % 16 == 0:
                    block = acc[pl.ds(pl.multiple_of(start + which * bit * rows, rows), rows), :]
                else:
                    upper = start + bit * rows
                    block = jnp.where(which == 0, acc[start : start + rows, :], acc[upper : upper + rows, :])
                ref[n] = block.astype(jnp.bfloat16)


def weight_grad(lefts, rights, place, bit, dp_count, earlier):
    rows, width = lefts[0].shape
    units = rights[0].shape[1]
    count, groups = len(lefts), len(rights)
    per = count // groups

    def part(g):
        return pl.BlockSpec((rows, units), lambda i, p: (jnp.clip(i - g * per, 0, per - 1), 0))

    pieces = dp_count // 2
    out_spec = pl.BlockSpec((pieces, width // dp_count, units), lambda i, p: (0, 0, 0), pipeline_mode=pl.Buffered(1))
    return pl.pallas_call(
        functools.partial(weight_kernel, count=count, groups=groups, bit=bit),
        grid_spec=pltpu.PrefetchScalarGridSpec(
            num_scalar_prefetch=1,
            grid=(count,),
            in_specs=[pl.BlockSpec((rows, width), lambda i, p: (0, 0))] * count
            + [part(g) for g in range(groups)]
            + [anywhere],
            out_specs=[out_spec] * 2,
            scratch_shapes=[pltpu.VMEM((width, units), jnp.float32)],
        ),
        out_shape=[jax.ShapeDtypeStruct((pieces, width // dp_count, units), jnp.bfloat16)] * 2,
        compiler_params=pltpu.CompilerParams(vmem_limit_bytes=vmem_bytes),
        cost_estimate=light,
        name="weight_grad",
    )(place, *lefts, *rights, earlier)


def order_kernel(value_ref, earlier_ref, out_ref):
    pass


def after(value, earlier):
    return pl.pallas_call(
        order_kernel,
        in_specs=[anywhere] * 2,
        out_specs=anywhere,
        out_shape=jax.ShapeDtypeStruct(value.shape, value.dtype),
        input_output_aliases={0: 0},
        name="after",
    )(value, earlier)


def call(kernel, outs, args, earlier, places=(), name=None, scratch=()):
    whole = lambda shape: pl.BlockSpec(shape, lambda i, *p: (0,) * len(shape))
    result = pl.pallas_call(
        kernel,
        grid_spec=pltpu.PrefetchScalarGridSpec(
            num_scalar_prefetch=len(places),
            grid=(1,),
            in_specs=[whole(a.shape) for a in args] + [anywhere],
            out_specs=[whole(o.shape) for o in outs],
            scratch_shapes=scratch,
        ),
        out_shape=outs,
        compiler_params=pltpu.CompilerParams(vmem_limit_bytes=vmem_bytes),
        cost_estimate=light,
        name=name,
    )(*places, *args, earlier)
    return result


def short(*shape):
    return jax.ShapeDtypeStruct(shape, jnp.bfloat16)


def added(first_ref, second_ref, n):
    return first_ref[n].astype(jnp.float32) + second_ref[n].astype(jnp.float32)


def split_kernel(place, kept_ref, came_ref, _, sent_out, kept_out):
    for n in range(sent_out.shape[0]):
        for out, which in ((sent_out, 1 - place[0]), (kept_out, place[0])):
            out[n] = added(kept_ref, came_ref, 2 * n + which).astype(out.dtype)


def split(kept, came, place, earlier):
    half = (kept.shape[0] // 2,) + kept.shape[1:]
    return call(split_kernel, [short(*half)] * 2, [kept, came], earlier, [place], "split")


def total_kernel(kept_ref, came_ref, _, out_ref):
    for n in range(out_ref.shape[0]):
        out_ref[n] = added(kept_ref, came_ref, n).astype(out_ref.dtype)


def total(kept, came, earlier, dtype=jnp.bfloat16):
    return call(total_kernel, [jax.ShapeDtypeStruct(kept.shape, dtype)], [kept, came], earlier, (), "total")[0]


def weave_kernel(place, own_ref, came_ref, _, out_ref):
    out_ref[place[0]] = own_ref[0]
    out_ref[1 - place[0]] = came_ref[0]


def weave(own, came, place, earlier):
    return call(weave_kernel, [short(2, *own.shape[1:])], [own, came], earlier, [place], "weave")[0]


def near_kernel(*refs, count):
    ins, outs = refs[: 2 * count], refs[2 * count + 1 :]
    for n in range(count):
        outs[n][...] = (ins[2 * n][...].astype(jnp.float32) + ins[2 * n + 1][...].astype(jnp.float32)).astype(outs[n].dtype)


def add_pairs(parts, earlier):
    evens = [o for o in sorted(parts) if o % 2 == 0]
    args = []
    for o in evens:
        args += [parts[o], swap(parts[o | 1], "mp", 1)]
    outs = [short(*parts[o].shape) for o in evens]
    result = call(functools.partial(near_kernel, count=len(evens)), outs, args, earlier, (), "add_pairs")
    return dict(zip(evens, result))


def middle_kernel(tok_ref, att_ref, weight_ref, gain_ref, _, mid_ref, normed_ref):
    middle = tok_ref[...].astype(jnp.float32) + dot(att_ref[...], weight_ref[...], 0, 0)
    inverse = lax.rsqrt(jnp.mean(middle * middle, axis=-1, keepdims=True) + norm_epsilon)
    mid_ref[...] = middle
    normed_ref[...] = (middle * inverse * gain_ref[...].astype(jnp.float32)).astype(jnp.bfloat16)


def norm_back(values, gain, grad_out):
    inverse = lax.rsqrt(jnp.mean(values * values, axis=-1, keepdims=True) + norm_epsilon)
    scaled = grad_out * gain
    mean_dot = jnp.mean(values * scaled, axis=-1, keepdims=True)
    return inverse * scaled - values * inverse * inverse * inverse * mean_dot, inverse


def branch_kernel(
    place, near_ref, came_ref, mid_ref, gain_ref, cot_ref, weight_ref, att_ref, _, grad_ref, branch_ref, sent_ref, kept_ref
):
    incoming = near_ref[...].astype(jnp.float32) + came_ref[...].astype(jnp.float32)
    middle = mid_ref[...]
    grad_mid, inverse = norm_back(middle, gain_ref[...].astype(jnp.float32), incoming)
    gain = jnp.sum(incoming * middle * inverse, axis=0, keepdims=True)
    grad_mid = cot_ref[...].astype(jnp.float32) + grad_mid
    grad_ref[...] = grad_mid
    branch = grad_mid.astype(jnp.bfloat16)
    branch_ref[...] = dot(weight_ref[...], branch, 1, 1).astype(jnp.bfloat16)
    half = sent_ref.shape[1]
    rest = att_ref.shape[0] - half
    for ref, which in ((sent_ref, 1 - place[0]), (kept_ref, place[0])):

        @pl.when(which == 0)
        def _():
            ref[0] = dot(att_ref[0:half, :], branch, 1, 0).astype(ref.dtype)

        @pl.when(which == 1)
        def _():
            ref[0, 0:rest, :] = dot(att_ref[half:, :], branch, 1, 0).astype(ref.dtype)
            line = lax.broadcasted_iota(jnp.int32, (half - rest, ref.shape[2]), 0) == 0
            ref[0, rest:, :] = jnp.where(line, gain, 0.0).astype(ref.dtype)


def output_kernel(mid_ref, near_ref, came_ref, _, out_ref):
    mlp = near_ref[...].astype(jnp.float32) + came_ref[...].astype(jnp.float32)
    out_ref[...] = (mid_ref[...] + mlp).astype(jnp.bfloat16)


def tokens_kernel(*refs, count):
    weight_ref, tok_ref, gain_ref, grad_ref, _, out_ref, rows = refs[count:]
    at = 0
    for ref in refs[:count]:
        rows[at : at + ref.shape[0], :] = ref[...]
        at += ref.shape[0]
    grad_normed = dot(rows[...], weight_ref[...], 0, 1)
    grad_in, _ = norm_back(tok_ref[...].astype(jnp.float32), gain_ref[...].astype(jnp.float32), grad_normed)
    out_ref[...] = grad_ref[...] + grad_in


def outer_kernel(place, left_ref, *refs):
    rights, out_ref = refs[:-2], refs[-1]
    half = out_ref.shape[1]
    left = left_ref[:, pl.ds(pl.multiple_of(place[0] * half, 128), half)]
    at = 0
    for ref in rights:
        out_ref[0, :, at : at + ref.shape[0]] = dot(left, ref[...], 0, 1).astype(out_ref.dtype)
        at += ref.shape[0]


def outer(place, left, rights, earlier):
    shape = short(1, left.shape[1] // 2, sum(r.shape[0] for r in rights))
    return call(outer_kernel, [shape], [left, *rights], earlier, [place], "outer")[0]


def near_keys_kernel(*refs, heads):
    ins, outs = refs[: 2 * heads], refs[2 * heads + 1 :]
    for h in range(heads):
        for n, out in enumerate(outs):
            both = added(ins[2 * h], ins[2 * h + 1], n)
            out[h * 2 * HEAD : (h + 1) * 2 * HEAD, :] = both.astype(jnp.bfloat16)


def merge_kernel(first_ref, second_ref, _, keys_out, values_out):
    both = (first_ref[...].astype(jnp.float32) + second_ref[...].astype(jnp.float32)).astype(jnp.bfloat16)
    for h in range(keys_out.shape[0] // HEAD):
        spot = slice(h * HEAD, (h + 1) * HEAD)
        keys_out[spot, :] = both[2 * h * HEAD : (2 * h + 1) * HEAD]
        values_out[spot, :] = both[(2 * h + 1) * HEAD : (2 * h + 2) * HEAD]


def finish_kernel(place, own_ref, other_ref, *refs, with_qkv, line_row):
    i = pl.program_id(0)
    steps = pl.num_programs(0)
    mine = (i * 2 // steps) == place[0]
    sums = jnp.where(mine, own_ref[0], other_ref[0]).astype(jnp.float32)
    if with_qkv:
        weight_ref, gain_ref, _, out_ref, line_ref, again_ref = refs
    else:
        _, out_ref, line_ref = refs

    out_ref[...] = sums
    if with_qkv:
        product = sums * weight_ref[...].astype(jnp.float32)
        again_ref[...] = jnp.sum(product, axis=1, keepdims=True) / gain_ref[...]

    @pl.when(i == steps - 1)
    def _():
        line_ref[...] = sums[line_row : line_row + 1]


def finish(place, own_rows, other_rows, width, earlier, extra=()):
    _, half, cols = own_rows.shape
    tile = min(256, half)
    per = half // tile
    own = pl.BlockSpec((1, tile, cols), lambda i, p: (0, jnp.where(i // per == p[0], i % per, 0), 0))
    far = pl.BlockSpec((1, tile, cols), lambda i, p: (0, jnp.where(i // per == p[0], 0, i % per), 0))
    row = lambda n: pl.BlockSpec((tile, n), lambda i, p: (i, 0))
    line = pl.BlockSpec((1, cols), lambda i, p: (0, 0))
    shape = lambda *s: jax.ShapeDtypeStruct(s, jnp.float32)
    return pl.pallas_call(
        functools.partial(finish_kernel, with_qkv=bool(extra), line_row=width % tile),
        grid_spec=pltpu.PrefetchScalarGridSpec(
            num_scalar_prefetch=1,
            grid=(2 * per,),
            in_specs=[own, far] + [row(a.shape[1]) for a in extra] + [anywhere],
            out_specs=[row(cols), line] + [row(1)] * (len(extra) // 2),
        ),
        out_shape=[shape(width, cols), shape(1, cols)] + [shape(width, 1)] * (len(extra) // 2),
        compiler_params=pltpu.CompilerParams(vmem_limit_bytes=vmem_bytes),
        cost_estimate=light,
        name="finish",
    )(place, own_rows, other_rows, *extra, earlier)


def layout(lengths, positions):
    segment = jnp.zeros_like(positions)
    begin = jnp.zeros_like(positions)
    end = jnp.int32(0)
    for n in range(lengths.shape[0]):
        end = end + lengths[n]
        later = positions >= end
        segment = segment + later.astype(jnp.int32)
        begin = jnp.where(later, end, begin)
    return (segment, positions - begin)


def swap(value, axis, bit):
    count = lax.axis_size(axis)
    return lax.ppermute(value, axis, [(i, i ^ bit) for i in range(count)])


def high_bits(count):
    bits, bit = [], 2
    while bit < count:
        bits.append(bit)
        bit *= 2
    return bits


def spread_far(value):
    blocks = {0: value}
    for bit in high_bits(lax.axis_size("mp")):
        for offset in sorted(blocks):
            blocks[offset | bit] = swap(blocks[offset], "mp", bit)
    return blocks


def wide(value):
    return value.astype(jnp.float32)


def wide(value):
    return value.astype(jnp.float32)


def last_pair(parts, earlier):
    parts = {o: parts[o] for o in parts if o % 2 == 0}
    bits = high_bits(lax.axis_size("mp"))
    for bit in bits[:-1]:
        parts = {o: total(parts[o][None], swap(parts[o | bit], "mp", bit)[None], earlier)[0] for o in parts if not o & bit}
    return parts[0], swap(parts[bits[-1]], "mp", bits[-1])


def copied(value, earlier):
    def kernel(value_ref, _, out_ref):
        out_ref[...] = value_ref[...]

    return call(kernel, [short(*value.shape)], [value], earlier, (), "copied")[0]


def all_bits(count):
    return [1] + high_bits(count) if count > 1 else []


def bit_of(axis, bit):
    return lax.rem(lax.axis_index(axis) // bit, 2)[None]


class Scatter:
    def __init__(self, parts):
        self.sent, self.kept = parts
        self.bits = all_bits(lax.axis_size("dp"))
        self.came = swap(self.sent, "dp", self.bits[0])

    def step(self, earlier):
        if not self.bits:
            return earlier
        self.bits = self.bits[1:]
        if not self.bits:
            self.result = total(self.kept, self.came, earlier, jnp.float32)[0]
            return self.result
        self.sent, self.kept = split(self.kept, self.came, bit_of("dp", self.bits[0]), earlier)
        self.came = swap(self.sent, "dp", self.bits[0])
        return self.kept


class Sum:
    def __init__(self, sent, kept):
        route = [("mp", b) for b in all_bits(lax.axis_size("mp"))] + [("dp", b) for b in all_bits(lax.axis_size("dp"))]
        self.down, self.up = route[1:], []
        self.kept = kept
        self.came = swap(sent, "mp", 1)

    def step(self, earlier):
        if self.done():
            return earlier
        if self.down is not None:
            while self.down:
                axis, bit = self.down.pop(0)
                rows = self.kept.shape[1] // 2
                if rows % 16:
                    self.kept = total(self.kept, self.came, earlier)
                    self.came = swap(self.kept, axis, bit)
                    return self.kept
                view = lambda v: v.reshape(2, rows, v.shape[2])
                self.up.append((axis, bit))
                sent, self.kept = split(view(self.kept), view(self.came), bit_of(axis, bit), earlier)
                self.came = swap(sent, axis, bit)
                return self.kept
            self.down = None
            self.kept = total(self.kept, self.came, earlier)
        else:
            axis, bit = self.up.pop()
            own = weave(self.kept, self.came, bit_of(axis, bit), earlier)
            self.kept = own.reshape(1, -1, own.shape[2])
        axis, bit = self.up[-1] if self.up else ("mp", 1)
        self.came = swap(self.kept, axis, bit)
        return self.kept

    def done(self):
        return self.down is None and not self.up


def on_device(
    tokens,
    seq_lengths,
    attn_gain,
    qkv_weight,
    qkv_bias,
    out_weight,
    mlp_gain,
    gate_weight,
    up_weight,
    down_weight,
    cotangent,
):
    tok_rows, width = tokens.shape
    mp_count = lax.axis_size("mp")
    mp_index = lax.axis_index("mp")
    q_rows = HEADS * HEAD
    lengths = seq_lengths[0]
    steps = jnp.arange(tok_rows, dtype=jnp.int32)
    segment, position = layout(lengths, mp_index * tok_rows + steps)
    key_rows = [(mp_index ^ o) * tok_rows + steps for o in range(mp_count)]
    key_segment, key_position = layout(lengths, jnp.concatenate(key_rows))
    bounds = jnp.stack([(mp_index * tok_rows - position[0]) // tok_rows, mp_index]).astype(jnp.int32)
    marks = jnp.arange(MARKS, dtype=jnp.int32)
    query_marks = (segment[None, :] != marks[:, None]).astype(jnp.bfloat16)
    key_marks = jnp.where(key_segment[:, None] == marks[None, :], masked_score, 0.0).astype(jnp.bfloat16)
    inverse_freq = rope_base ** (-2.0 * jnp.arange(HEAD // 2, dtype=jnp.float32) / HEAD)
    key_angles = inverse_freq[:, None] * key_position.astype(jnp.float32)[None, :]
    cos_keys, sin_keys = jnp.cos(key_angles), jnp.sin(key_angles)

    normed, queries, own_kv = project(tokens, attn_gain, qkv_weight, qkv_bias, cos_keys, sin_keys)
    blocks = spread_far(own_kv)
    blocks.update({o | 1: swap(blocks[o], "mp", 1) for o in sorted(blocks)})
    blocks = [blocks[o] for o in range(mp_count)]

    cot = copied(cotangent, blocks[2])
    cots = spread_far(cot)
    cots[1] = swap(cotangent, "mp", 1)
    attended, log_totals = attend(bounds, queries, query_marks, key_marks, blocks, cot)
    for o in range(2, mp_count, 2):
        cots[o | 1] = swap(cots[o], "mp", 1)

    middle, normed_mid = call(
        middle_kernel,
        [jax.ShapeDtypeStruct((tok_rows, width), jnp.float32), short(tok_rows, width)],
        [tokens, attended, out_weight, mlp_gain[None]],
        cot,
        name="middle",
    )
    gate_t, up_t = gate_weight.T, up_weight.T
    mids = {0: normed_mid, 1: swap(normed_mid, "mp", 1)}
    mids.update(spread_far(normed_mid))
    outs, grads, hids, ggs, gus = {}, {}, [], [], []
    clock = normed_mid
    for o in range(0, mp_count, 2):
        if o:
            mids[o] = after(mids[o], clock)
            mids[o | 1] = swap(mids[o], "mp", 1)
        pair = [o, o | 1]
        out, grad, hid, gg, gu = feed_forward(
            [mids[k] for k in pair], [cots[k] for k in pair], gate_t, up_t, down_weight, clock
        )
        clock = hid
        hids.append(hid), ggs.append(gg), gus.append(gu)
        for k in (0, 1):
            outs[o | k], grads[o | k] = out[k], grad[k]
    xs = [mids[o] for o in range(mp_count)]
    cs = [cots[o] for o in range(mp_count)]

    near_grads = add_pairs(grads, clock)
    clock = near_grads[0]
    dp_count = lax.axis_size("dp")
    low = bit_of("dp", 1)
    wide_down = weight_grad(cs, hids, low, 1, dp_count, clock)
    near_outs = add_pairs(outs, wide_down[0])
    wide_gate = weight_grad(xs, ggs, low, 1, dp_count, near_outs[0])
    wide_up = weight_grad(xs, gus, low, 1, dp_count, wide_gate[0])
    down_sum, gate_sum, up_sum = Scatter(wide_down), Scatter(wide_gate), Scatter(wide_up)
    clock = wide_up[0]
    near_outs = {o: after(near_outs[o], clock) if o else near_outs[o] for o in near_outs}
    outs = last_pair(near_outs, clock)
    core = bit_of("mp", 1)
    half = normed.shape[1] // 2
    grad_middle, grad_attended, *out_halves = call(
        branch_kernel,
        [jax.ShapeDtypeStruct((tok_rows, width), jnp.float32), short(q_rows, tok_rows), short(1, half, width), short(1, half, width)],
        [*last_pair(near_grads, clock), middle, mlp_gain[None], cotangent, out_weight, attended],
        clock,
        [core],
        "branch",
    )
    out_sum = Sum(*out_halves)
    clock = down_sum.step(grad_attended)
    back = functools.partial(
        attend_back,
        bounds=bounds,
        q=queries,
        query_marks=query_marks,
        key_marks=key_marks,
        o=attended,
        go=grad_attended,
        log=log_totals,
        cos_table=cos_keys,
        sin_table=sin_keys,
        blocks=blocks,
    )
    grad_qs, kv_pairs = [], []
    for head in range(KV_HEADS):
        grad_q, kv_even, kv_odd = back(head, earlier=clock)
        grad_qs.append(grad_q)
        kv_pairs += [kv_even, swap(kv_odd, "mp", 1)]
        clock = out_sum.step(grad_q)
        clock = (up_sum if head else gate_sum).step(clock)
        if head == 0:
            clock = down_sum.step(clock)
            output = clock = call(output_kernel, [short(tok_rows, width)], [middle, *outs], clock, name="output")[0]
    near_kv = call(
        functools.partial(near_keys_kernel, heads=KV_HEADS),
        [short(KV_HEADS * 2 * HEAD, tok_rows)] * (mp_count // 2),
        kv_pairs,
        clock,
        name="near_keys",
    )
    kv_sums = last_pair({2 * n: a for n, a in enumerate(near_kv)}, near_kv[0])
    clock = gate_sum.step(near_kv[0])
    clock = down_sum.step(clock)
    grad_keys, grad_values = call(merge_kernel, [short(KV_HEADS * HEAD, tok_rows)] * 2, kv_sums, clock, name="merge")
    rows = [*grad_qs, grad_keys, grad_values]
    sent = outer(1 - core, normed, rows, grad_keys)
    kept = outer(core, normed, rows, sent)
    qkv_sum = Sum(sent, kept)

    clock = out_sum.step(kept)
    clock = qkv_sum.step(clock)
    grad_tokens = clock = call(
        functools.partial(tokens_kernel, count=len(rows)),
        [jax.ShapeDtypeStruct((tok_rows, width), jnp.float32)],
        [*rows, qkv_weight, tokens, attn_gain[None], grad_middle],
        clock,
        name="tokens",
        scratch=[pltpu.VMEM((qkv_weight.shape[1], tok_rows), jnp.bfloat16)],
    )[0]
    for item in (up_sum, out_sum, gate_sum, out_sum, qkv_sum, out_sum, up_sum):
        clock = item.step(clock)
    for item in (down_sum, gate_sum, up_sum) * 8:
        clock = item.step(clock)
    while not out_sum.done():
        clock = out_sum.step(qkv_sum.step(clock))
    grad_out_weight, gain_line = finish(core, out_sum.kept, out_sum.came, width, clock)
    clock = gain_line
    while not qkv_sum.done():
        clock = qkv_sum.step(clock)
    grad_qkv_weight, bias_line, grad_attn_gain = finish(
        core, qkv_sum.kept, qkv_sum.came, width, clock, [qkv_weight, wide(attn_gain)[:, None]]
    )

    return (
        output,
        grad_tokens,
        grad_attn_gain[:, 0],
        grad_qkv_weight,
        bias_line[0],
        grad_out_weight,
        gain_line[0],
        gate_sum.result,
        up_sum.result,
        down_sum.result.T,
    )


def solution(mesh):
    return jax.shard_map(
        on_device,
        mesh=mesh,
        in_specs=(
            P(("dp", "mp"), None),
            P("dp", None),
            P(),
            P(),
            P(),
            P(),
            P(),
            P(None, "mp"),
            P(None, "mp"),
            P("mp", None),
            P(("dp", "mp"), None),
        ),
        out_specs=(
            P(("dp", "mp"), None),
            P(("dp", "mp"), None),
            P(),
            P(),
            P(),
            P(),
            P(),
            P("dp", "mp"),
            P("dp", "mp"),
            P("mp", "dp"),
        ),
        check_vma=False,
    )
```

```python
import functools

import jax
import jax.numpy as jnp
from jax import lax
from jax.experimental import pallas as pl
from jax.experimental.pallas import tpu as pltpu
from jax.sharding import PartitionSpec as P

HEADS = 14
KV_HEADS = 2
HEAD = 64
MARKS = 16

norm_epsilon = 1e-06
rope_base = 1000000.0
masked_score = -1e30
vmem_bytes = 52 * 2**20


anywhere = pl.BlockSpec(memory_space=pltpu.HBM)
light = pl.CostEstimate(flops=1000, bytes_accessed=1000, transcendentals=0)


def dot(left, right, left_dim, right_dim):
    return lax.dot_general(
        left, right, (((left_dim,), (right_dim,)), ((), ())), preferred_element_type=jnp.float32
    )


def causal(tile):
    key_id = lax.broadcasted_iota(jnp.int32, tile.shape, 0)
    query_id = lax.broadcasted_iota(jnp.int32, tile.shape, 1)
    return jnp.where(key_id <= query_id, tile, masked_score)


def turn(values, cos_table, sin_table):
    half = HEAD // 2
    pieces = []
    for row in range(0, values.shape[0], HEAD):
        lower, upper = values[row : row + half], values[row + half : row + HEAD]
        pieces += [lower * cos_table - upper * sin_table, upper * cos_table + lower * sin_table]
    return pieces


def project_kernel(tok_ref, gain_ref, weight_ref, bias_ref, cos_ref, sin_ref, normed_ref, q_ref, kv_ref):
    values = tok_ref[...].astype(jnp.float32)
    inverse = lax.rsqrt(jnp.mean(values * values, axis=-1, keepdims=True) + norm_epsilon)
    normed = (values * inverse * gain_ref[...].astype(jnp.float32)).astype(jnp.bfloat16)
    rows, width = normed.shape
    normed_ref[:, 0:width] = normed
    ones_at = lax.broadcasted_iota(jnp.int32, (rows, normed_ref.shape[1] - width), 1) == 0
    normed_ref[:, width:] = jnp.where(ones_at, 1.0, 0.0).astype(jnp.bfloat16)
    cos_table, sin_table = cos_ref[:, 0:rows], sin_ref[:, 0:rows]
    q_width, kv_width, half = HEADS * HEAD, KV_HEADS * HEAD, HEAD // 2
    step = 128
    for lo in range(0, weight_ref.shape[1], step):
        cols = slice(lo, lo + step)
        part = dot(normed, weight_ref[:, cols], 1, 0) + bias_ref[:, cols].astype(jnp.float32)
        part = part.T
        if lo < q_width + kv_width:
            pieces = turn(part, cos_table, sin_table)
        else:
            pieces = [part[r : r + half] for r in range(0, step, half)]
        for n, piece in enumerate(pieces):
            row = lo + n * half
            piece = piece.astype(jnp.bfloat16)
            if row < q_width:
                q_ref[row : row + half, :] = piece * jnp.bfloat16(HEAD ** (-0.5))
            else:
                row -= q_width
                which, row = row // kv_width, row % kv_width
                head, row = row // HEAD, row % HEAD
                place = (2 * head + which) * HEAD + row
                kv_ref[place : place + half, :] = piece


def project(tokens, gain, weight, bias, cos_table, sin_table):
    rows, width = tokens.shape
    shape = lambda *s: jax.ShapeDtypeStruct(s, jnp.bfloat16)
    return pl.pallas_call(
        project_kernel,
        out_shape=[shape(rows, width + 128), shape(HEADS * HEAD, rows), shape(2 * KV_HEADS * HEAD, rows)],
        compiler_params=pltpu.CompilerParams(vmem_limit_bytes=vmem_bytes),
        cost_estimate=light,
        name="project",
    )(tokens, gain[None], weight, bias[None], cos_table, sin_table)


def load_keys(blocks, marks_ref, kx, vx, vk):
    rows = blocks[0].shape[1]
    for o, block in enumerate(blocks):
        spot = slice(o * rows, (o + 1) * rows)
        flat = block[...].astype(jnp.float32).T.astype(jnp.bfloat16)
        kx[spot, 0:HEAD] = flat[:, 0:HEAD]
        if vk is not None:
            vk[spot, :] = flat[:, HEAD:]
        if vx is not None:
            vx[0:HEAD, spot] = block[HEAD:, :]
    kx[:, HEAD:] = marks_ref[...]
    if vx is not None:
        vx[HEAD:, :] = jnp.ones((MARKS, vx.shape[1]), jnp.bfloat16)


def staged(items, begin, finish):
    earlier = None
    for item in items:
        state = begin(item)
        if earlier is not None:
            finish(*earlier)
        earlier = (item, state)
    finish(*earlier)


def attend_kernel(bounds, q_ref, mark_ref, marks_ref, *refs, count):
    blocks = refs[:count]
    out_ref, log_ref, kx, vx, q_ext, acc, top = refs[-7:]
    rows = q_ref.shape[1]
    half = rows // 2
    heads = q_ref.shape[0] // HEAD
    load_keys(blocks, marks_ref, kx, vx, None)
    for h in range(heads):
        q_ext[h, 0:HEAD, :] = q_ref[h * HEAD : (h + 1) * HEAD, :]
        q_ext[h, HEAD:, :] = mark_ref[...]
    acc[...] = jnp.zeros_like(acc)
    top[...] = jnp.full_like(top, 2 * masked_score)

    def begin(item):
        h, start, size, lo, hi, diag = item
        scores = dot(kx[pl.ds(start, size), :], q_ext[h, :, lo:hi], 1, 0)
        return causal(scores) if diag else scores

    def finish(item, scores):
        h, start, size, lo, hi, diag = item
        old = top[h, :, lo:hi]
        new = jnp.maximum(old, jnp.max(scores, axis=0, keepdims=True))
        weights = jnp.exp(scores - new).astype(jnp.bfloat16)
        top[h, :, lo:hi] = new
        acc[h, :, lo:hi] = acc[h, :, lo:hi] * jnp.exp(old - new) + dot(vx[:, pl.ds(start, size)], weights, 1, 0)

    first, own = bounds[0], bounds[1]

    def whole(c, carry):
        start = pl.multiple_of((c ^ own) * rows, rows)
        staged([(h, start, rows, 0, rows, False) for h in range(heads)], begin, finish)
        return carry

    lax.fori_loop(first, own, whole, 0)
    spots = [(0, half, half, rows, False), (0, half, 0, half, True), (half, half, half, rows, True)]
    staged([(h,) + spot for h in range(heads) for spot in spots], begin, finish)
    for h in range(heads):
        total = acc[h, HEAD : HEAD + 1, :]
        out_ref[h * HEAD : (h + 1) * HEAD, :] = (acc[h, 0:HEAD, :] / total).astype(jnp.bfloat16)
        log_ref[h] = top[h] + jnp.log(total)


def attend(bounds, q, query_marks, key_marks, blocks, earlier):
    width, rows = q.shape
    heads = width // HEAD
    rep = heads // KV_HEADS
    group = key_marks.shape[0]
    whole = lambda a: pl.BlockSpec(a.shape, lambda g, b: (0, 0))
    by_head = lambda n: pl.BlockSpec((n, rows), lambda g, b: (g, 0))
    return pl.pallas_call(
        functools.partial(attend_kernel, count=len(blocks)),
        grid_spec=pltpu.PrefetchScalarGridSpec(
            num_scalar_prefetch=1,
            grid=(KV_HEADS,),
            in_specs=[by_head(rep * HEAD), whole(query_marks), whole(key_marks)] + [by_head(2 * HEAD)] * len(blocks) + [anywhere],
            out_specs=[by_head(rep * HEAD), pl.BlockSpec((rep, 1, rows), lambda g, b: (g, 0, 0))],
            scratch_shapes=[
                pltpu.VMEM((group, HEAD + MARKS), jnp.bfloat16),
                pltpu.VMEM((HEAD + MARKS, group), jnp.bfloat16),
                pltpu.VMEM((rep, HEAD + MARKS, rows), jnp.bfloat16),
                pltpu.VMEM((rep, HEAD + MARKS, rows), jnp.float32),
                pltpu.VMEM((rep, 1, rows), jnp.float32),
            ],
        ),
        out_shape=[
            jax.ShapeDtypeStruct((width, rows), jnp.bfloat16),
            jax.ShapeDtypeStruct((heads, 1, rows), jnp.float32),
        ],
        compiler_params=pltpu.CompilerParams(vmem_limit_bytes=vmem_bytes),
        cost_estimate=light,
        name="attend",
    )(bounds, q, query_marks, key_marks, *blocks, earlier)


def attend_back_kernel(
    bounds, q_ref, mark_ref, marks_ref, o_ref, go_ref, log_ref, cos_ref, sin_ref, *refs, count
):
    blocks = refs[:count]
    refs = refs[count + 1 :]
    gq_ref = refs[0]
    gkv_refs = refs[1:3]
    kx, vk, q_ext, acc, delta, gkv = refs[3:]
    rows = q_ref.shape[1]
    half = rows // 2
    heads = q_ref.shape[0] // HEAD
    load_keys(blocks, marks_ref, kx, None, vk)
    for h in range(heads):
        spot = slice(h * HEAD, (h + 1) * HEAD)
        q_ext[h, 0:HEAD, :] = q_ref[spot, :]
        q_ext[h, HEAD:, :] = mark_ref[...]
        product = o_ref[spot, :].astype(jnp.float32) * go_ref[spot, :].astype(jnp.float32)
        delta[h] = jnp.sum(product, axis=0, keepdims=True)
    acc[...] = jnp.zeros_like(acc)
    gkv[...] = jnp.zeros_like(gkv)

    def begin(item):
        h, start, size, lo, hi, diag, keys_t = item
        scores = dot(kx[pl.ds(start, size), :], q_ext[h, :, lo:hi], 1, 0)
        grad_prob = dot(vk[pl.ds(start, size), :], go_ref[h * HEAD : (h + 1) * HEAD, lo:hi], 1, 0)
        return (causal(scores) if diag else scores), grad_prob

    def finish(item, state):
        h, start, size, lo, hi, diag, keys_t = item
        scores, grad_prob = state
        spot = slice(h * HEAD, (h + 1) * HEAD)
        prob = jnp.exp(scores - log_ref[h, :, lo:hi])
        grad_score = (prob * (grad_prob - delta[h, :, lo:hi])).astype(jnp.bfloat16)
        gkv[HEAD:, pl.ds(start, size)] += dot(go_ref[spot, lo:hi], prob.astype(jnp.bfloat16), 1, 1)
        gkv[0:HEAD, pl.ds(start, size)] += dot(q_ref[spot, lo:hi], grad_score, 1, 1)
        acc[h, :, lo:hi] += dot(keys_t, grad_score, 1, 0)

    first, own = bounds[0], bounds[1]
    for o in range(1, count):
        c = own ^ o

        @pl.when((c >= first) & (c < own))
        def _():
            keys_t = blocks[o][0:HEAD, :]
            staged([(h, o * rows, rows, 0, rows, False, keys_t) for h in range(heads)], begin, finish)

    low, high = blocks[0][0:HEAD, 0:half], blocks[0][0:HEAD, half:]
    spots = [(0, half, half, rows, False, low), (0, half, 0, half, True, low), (half, half, half, rows, True, high)]
    staged([(h,) + spot for h in range(heads) for spot in spots], begin, finish)
    cos_own, sin_own = cos_ref[:, 0:rows], -sin_ref[:, 0:rows]
    for h in range(heads):
        pieces = turn(acc[h] * (HEAD ** (-0.5)), cos_own, sin_own)
        for n, piece in enumerate(pieces):
            row = h * HEAD + n * (HEAD // 2)
            gq_ref[row : row + HEAD // 2, :] = piece.astype(jnp.bfloat16)
    for o in range(count):
        spot = slice(o * rows, (o + 1) * rows)
        pieces = turn(gkv[0:HEAD, spot], cos_ref[:, spot], -sin_ref[:, spot])
        for n, piece in enumerate(pieces):
            gkv_refs[o % 2][o // 2, n * (HEAD // 2) : (n + 1) * (HEAD // 2), :] = piece.astype(jnp.bfloat16)
        gkv_refs[o % 2][o // 2, HEAD:, :] = gkv[HEAD:, spot].astype(jnp.bfloat16)


def attend_back(head, bounds, q, query_marks, key_marks, o, go, log, cos_table, sin_table, blocks, earlier):
    width, rows = q.shape
    rep = HEADS // KV_HEADS
    group = key_marks.shape[0]
    count = len(blocks)
    whole = lambda a: pl.BlockSpec(a.shape, lambda i, b: (0, 0))
    by_head = lambda n: pl.BlockSpec((n, rows), lambda i, b: (head, 0))
    return pl.pallas_call(
        functools.partial(attend_back_kernel, count=count),
        grid_spec=pltpu.PrefetchScalarGridSpec(
            num_scalar_prefetch=1,
            grid=(1,),
            in_specs=[by_head(rep * HEAD), whole(query_marks), whole(key_marks), by_head(rep * HEAD), by_head(rep * HEAD)]
            + [pl.BlockSpec((rep, 1, rows), lambda i, b: (head, 0, 0)), whole(cos_table), whole(sin_table)]
            + [by_head(2 * HEAD)] * count
            + [anywhere],
            out_specs=[pl.BlockSpec((rep * HEAD, rows), lambda i, b: (0, 0))]
            + [pl.BlockSpec((count // 2, 2 * HEAD, rows), lambda i, b: (0, 0, 0))] * 2,
            scratch_shapes=[
                pltpu.VMEM((group, HEAD + MARKS), jnp.bfloat16),
                pltpu.VMEM((group, HEAD), jnp.bfloat16),
                pltpu.VMEM((rep, HEAD + MARKS, rows), jnp.bfloat16),
                pltpu.VMEM((rep, HEAD, rows), jnp.float32),
                pltpu.VMEM((rep, 1, rows), jnp.float32),
                pltpu.VMEM((2 * HEAD, group), jnp.float32),
            ],
        ),
        out_shape=[jax.ShapeDtypeStruct((rep * HEAD, rows), jnp.bfloat16)]
        + [jax.ShapeDtypeStruct((count // 2, 2 * HEAD, rows), jnp.bfloat16)] * 2,
        compiler_params=pltpu.CompilerParams(vmem_limit_bytes=vmem_bytes),
        cost_estimate=light,
        name="attend_back",
    )(bounds, q, query_marks, key_marks, o, go, log, cos_table, sin_table, *blocks, earlier)


def act_kernel(*refs, count, steps):
    xs, cots = refs[:count], refs[count : 2 * count]
    gate_ref, up_ref, down_ref = refs[2 * count : 2 * count + 3]
    refs = refs[2 * count + 4 :]
    outs, grads = refs[:count], refs[count : 2 * count]
    hid_ref, gg_ref, gu_ref = refs[2 * count :]
    i = pl.program_id(0)

    def run(n):
        x = xs[n][...]
        gate = dot(x, gate_ref[...], 1, 1)
        up = dot(x, up_ref[...], 1, 1)
        grad_hidden = dot(cots[n][...], down_ref[...], 1, 1)
        sig = jax.nn.sigmoid(gate)
        silu = gate * sig
        hidden = (silu * up).astype(jnp.bfloat16)
        grad_gate = (grad_hidden * up * (sig * (1.0 + gate * (1.0 - sig)))).astype(jnp.bfloat16)
        grad_up = (grad_hidden * silu).astype(jnp.bfloat16)
        hid_ref[...] = hidden
        gg_ref[...] = grad_gate
        gu_ref[...] = grad_up
        grads[n][...] = (dot(grad_gate, gate_ref[...], 1, 0) + dot(grad_up, up_ref[...], 1, 0)).astype(jnp.bfloat16)
        outs[n][...] = dot(hidden, down_ref[...], 1, 0).astype(jnp.bfloat16)

    for n in range(count):
        pl.when(i // steps == n)(functools.partial(run, n))


def feed_forward(xs, cots, gate_t, up_t, down_weight, earlier):
    rows, width = xs[0].shape
    units = gate_t.shape[0]
    count = len(xs)
    tile = min(256, rows)
    steps = rows // tile

    def chunk(n):
        return pl.BlockSpec((tile, width), lambda i: (jnp.clip(i - n * steps, 0, steps - 1), 0))

    whole = lambda w: pl.BlockSpec(w.shape, lambda i: (0, 0), pipeline_mode=pl.Buffered(1))
    by_rows = pl.BlockSpec((tile, units), lambda i: (i, 0))
    small = jax.ShapeDtypeStruct((rows, width), jnp.bfloat16)
    large = jax.ShapeDtypeStruct((count * rows, units), jnp.bfloat16)
    result = pl.pallas_call(
        functools.partial(act_kernel, count=count, steps=steps),
        grid=(count * steps,),
        in_specs=[chunk(n) for n in range(count)] * 2 + [whole(gate_t), whole(up_t), whole(down_weight), anywhere],
        out_specs=[chunk(n) for n in range(count)] * 2 + [by_rows] * 3,
        out_shape=[small] * (2 * count) + [large] * 3,
        compiler_params=pltpu.CompilerParams(vmem_limit_bytes=vmem_bytes),
        cost_estimate=light,
        name="feed_forward",
    )(*xs, *cots, gate_t, up_t, down_weight, earlier)
    return result[:count], result[count : 2 * count], *result[2 * count :]


def weight_kernel(place, *refs, count, groups, bit):
    lefts, rights = refs[:count], refs[count : count + groups]
    sent_ref, kept_ref, acc = refs[-3:]
    i = pl.program_id(0)

    for n in range(count):

        @pl.when(i == n)
        def _():
            product = dot(lefts[n][...], rights[n * groups // count][...], 0, 0)
            acc[...] = product if n == 0 else acc[...] + product

    @pl.when(i == count - 1)
    def _():
        pieces, rows, _ = sent_ref.shape
        for ref, which in ((sent_ref, 1 - place[0]), (kept_ref, place[0])):
            for n in range(pieces):
                low, high = n % bit, n // bit
                start = (high * 2 * bit + low) * rows
                if rows % 16 == 0:
                    block = acc[pl.ds(pl.multiple_of(start + which * bit * rows, rows), rows), :]
                else:
                    upper = start + bit * rows
                    block = jnp.where(which == 0, acc[start : start + rows, :], acc[upper : upper + rows, :])
                ref[n] = block.astype(jnp.bfloat16)


def weight_grad(lefts, rights, place, bit, dp_count, earlier):
    rows, width = lefts[0].shape
    units = rights[0].shape[1]
    count, groups = len(lefts), len(rights)
    per = count // groups

    def part(g):
        return pl.BlockSpec((rows, units), lambda i, p: (jnp.clip(i - g * per, 0, per - 1), 0))

    pieces = dp_count // 2
    out_spec = pl.BlockSpec((pieces, width // dp_count, units), lambda i, p: (0, 0, 0), pipeline_mode=pl.Buffered(1))
    return pl.pallas_call(
        functools.partial(weight_kernel, count=count, groups=groups, bit=bit),
        grid_spec=pltpu.PrefetchScalarGridSpec(
            num_scalar_prefetch=1,
            grid=(count,),
            in_specs=[pl.BlockSpec((rows, width), lambda i, p: (0, 0))] * count
            + [part(g) for g in range(groups)]
            + [anywhere],
            out_specs=[out_spec] * 2,
            scratch_shapes=[pltpu.VMEM((width, units), jnp.float32)],
        ),
        out_shape=[jax.ShapeDtypeStruct((pieces, width // dp_count, units), jnp.bfloat16)] * 2,
        compiler_params=pltpu.CompilerParams(vmem_limit_bytes=vmem_bytes),
        cost_estimate=light,
        name="weight_grad",
    )(place, *lefts, *rights, earlier)


def order_kernel(value_ref, earlier_ref, out_ref):
    pass


def after(value, earlier):
    return pl.pallas_call(
        order_kernel,
        in_specs=[anywhere] * 2,
        out_specs=anywhere,
        out_shape=jax.ShapeDtypeStruct(value.shape, value.dtype),
        input_output_aliases={0: 0},
        name="after",
    )(value, earlier)


def call(kernel, outs, args, earlier, places=(), name=None, scratch=()):
    whole = lambda shape: pl.BlockSpec(shape, lambda i, *p: (0,) * len(shape))
    result = pl.pallas_call(
        kernel,
        grid_spec=pltpu.PrefetchScalarGridSpec(
            num_scalar_prefetch=len(places),
            grid=(1,),
            in_specs=[whole(a.shape) for a in args] + [anywhere],
            out_specs=[whole(o.shape) for o in outs],
            scratch_shapes=scratch,
        ),
        out_shape=outs,
        compiler_params=pltpu.CompilerParams(vmem_limit_bytes=vmem_bytes),
        cost_estimate=light,
        name=name,
    )(*places, *args, earlier)
    return result


def short(*shape):
    return jax.ShapeDtypeStruct(shape, jnp.bfloat16)


def added(first_ref, second_ref, n):
    return first_ref[n].astype(jnp.float32) + second_ref[n].astype(jnp.float32)


def split_kernel(place, kept_ref, came_ref, _, sent_out, kept_out):
    for n in range(sent_out.shape[0]):
        for out, which in ((sent_out, 1 - place[0]), (kept_out, place[0])):
            out[n] = added(kept_ref, came_ref, 2 * n + which).astype(out.dtype)


def split(kept, came, place, earlier):
    half = (kept.shape[0] // 2,) + kept.shape[1:]
    return call(split_kernel, [short(*half)] * 2, [kept, came], earlier, [place], "split")


def total_kernel(kept_ref, came_ref, _, out_ref):
    for n in range(out_ref.shape[0]):
        out_ref[n] = added(kept_ref, came_ref, n).astype(out_ref.dtype)


def total(kept, came, earlier, dtype=jnp.bfloat16):
    return call(total_kernel, [jax.ShapeDtypeStruct(kept.shape, dtype)], [kept, came], earlier, (), "total")[0]


def weave_kernel(place, own_ref, came_ref, _, out_ref):
    out_ref[place[0]] = own_ref[0]
    out_ref[1 - place[0]] = came_ref[0]


def weave(own, came, place, earlier):
    return call(weave_kernel, [short(2, *own.shape[1:])], [own, came], earlier, [place], "weave")[0]


def near_kernel(*refs, count):
    ins, outs = refs[: 2 * count], refs[2 * count + 1 :]
    for n in range(count):
        outs[n][...] = (ins[2 * n][...].astype(jnp.float32) + ins[2 * n + 1][...].astype(jnp.float32)).astype(outs[n].dtype)


def add_pairs(parts, earlier):
    evens = [o for o in sorted(parts) if o % 2 == 0]
    args = []
    for o in evens:
        args += [parts[o], swap(parts[o | 1], "mp", 1)]
    outs = [short(*parts[o].shape) for o in evens]
    result = call(functools.partial(near_kernel, count=len(evens)), outs, args, earlier, (), "add_pairs")
    return dict(zip(evens, result))


def middle_kernel(tok_ref, att_ref, weight_ref, gain_ref, _, mid_ref, normed_ref):
    middle = tok_ref[...].astype(jnp.float32) + dot(att_ref[...], weight_ref[...], 0, 0)
    inverse = lax.rsqrt(jnp.mean(middle * middle, axis=-1, keepdims=True) + norm_epsilon)
    mid_ref[...] = middle
    normed_ref[...] = (middle * inverse * gain_ref[...].astype(jnp.float32)).astype(jnp.bfloat16)


def norm_back(values, gain, grad_out):
    inverse = lax.rsqrt(jnp.mean(values * values, axis=-1, keepdims=True) + norm_epsilon)
    scaled = grad_out * gain
    mean_dot = jnp.mean(values * scaled, axis=-1, keepdims=True)
    return inverse * scaled - values * inverse * inverse * inverse * mean_dot, inverse


def branch_kernel(
    place, near_ref, came_ref, mid_ref, gain_ref, cot_ref, weight_ref, att_ref, _, grad_ref, branch_ref, sent_ref, kept_ref
):
    incoming = near_ref[...].astype(jnp.float32) + came_ref[...].astype(jnp.float32)
    middle = mid_ref[...]
    grad_mid, inverse = norm_back(middle, gain_ref[...].astype(jnp.float32), incoming)
    gain = jnp.sum(incoming * middle * inverse, axis=0, keepdims=True)
    grad_mid = cot_ref[...].astype(jnp.float32) + grad_mid
    grad_ref[...] = grad_mid
    branch = grad_mid.astype(jnp.bfloat16)
    branch_ref[...] = dot(weight_ref[...], branch, 1, 1).astype(jnp.bfloat16)
    half = sent_ref.shape[1]
    rest = att_ref.shape[0] - half
    for ref, which in ((sent_ref, 1 - place[0]), (kept_ref, place[0])):

        @pl.when(which == 0)
        def _():
            ref[0] = dot(att_ref[0:half, :], branch, 1, 0).astype(ref.dtype)

        @pl.when(which == 1)
        def _():
            ref[0, 0:rest, :] = dot(att_ref[half:, :], branch, 1, 0).astype(ref.dtype)
            line = lax.broadcasted_iota(jnp.int32, (half - rest, ref.shape[2]), 0) == 0
            ref[0, rest:, :] = jnp.where(line, gain, 0.0).astype(ref.dtype)


def output_kernel(mid_ref, near_ref, came_ref, _, out_ref):
    mlp = near_ref[...].astype(jnp.float32) + came_ref[...].astype(jnp.float32)
    out_ref[...] = (mid_ref[...] + mlp).astype(jnp.bfloat16)


def tokens_kernel(*refs, count):
    weight_ref, tok_ref, gain_ref, grad_ref, _, out_ref, rows = refs[count:]
    at = 0
    for ref in refs[:count]:
        rows[at : at + ref.shape[0], :] = ref[...]
        at += ref.shape[0]
    grad_normed = dot(rows[...], weight_ref[...], 0, 1)
    grad_in, _ = norm_back(tok_ref[...].astype(jnp.float32), gain_ref[...].astype(jnp.float32), grad_normed)
    out_ref[...] = grad_ref[...] + grad_in


def outer_kernel(place, left_ref, *refs):
    rights, out_ref = refs[:-2], refs[-1]
    half = out_ref.shape[1]
    left = left_ref[:, pl.ds(pl.multiple_of(place[0] * half, 128), half)]
    at = 0
    for ref in rights:
        out_ref[0, :, at : at + ref.shape[0]] = dot(left, ref[...], 0, 1).astype(out_ref.dtype)
        at += ref.shape[0]


def outer(place, left, rights, earlier):
    shape = short(1, left.shape[1] // 2, sum(r.shape[0] for r in rights))
    return call(outer_kernel, [shape], [left, *rights], earlier, [place], "outer")[0]


def near_keys_kernel(*refs, heads):
    ins, outs = refs[: 2 * heads], refs[2 * heads + 1 :]
    for h in range(heads):
        for n, out in enumerate(outs):
            both = added(ins[2 * h], ins[2 * h + 1], n)
            out[h * 2 * HEAD : (h + 1) * 2 * HEAD, :] = both.astype(jnp.bfloat16)


def merge_kernel(first_ref, second_ref, _, keys_out, values_out):
    both = (first_ref[...].astype(jnp.float32) + second_ref[...].astype(jnp.float32)).astype(jnp.bfloat16)
    for h in range(keys_out.shape[0] // HEAD):
        spot = slice(h * HEAD, (h + 1) * HEAD)
        keys_out[spot, :] = both[2 * h * HEAD : (2 * h + 1) * HEAD]
        values_out[spot, :] = both[(2 * h + 1) * HEAD : (2 * h + 2) * HEAD]


def finish_kernel(place, own_ref, other_ref, *refs, with_qkv, line_row):
    i = pl.program_id(0)
    steps = pl.num_programs(0)
    mine = (i * 2 // steps) == place[0]
    sums = jnp.where(mine, own_ref[0], other_ref[0]).astype(jnp.float32)
    if with_qkv:
        weight_ref, gain_ref, _, out_ref, line_ref, again_ref = refs
    else:
        _, out_ref, line_ref = refs

    out_ref[...] = sums
    if with_qkv:
        product = sums * weight_ref[...].astype(jnp.float32)
        again_ref[...] = jnp.sum(product, axis=1, keepdims=True) / gain_ref[...]

    @pl.when(i == steps - 1)
    def _():
        line_ref[...] = sums[line_row : line_row + 1]


def finish(place, own_rows, other_rows, width, earlier, extra=()):
    _, half, cols = own_rows.shape
    tile = min(256, half)
    per = half // tile
    own = pl.BlockSpec((1, tile, cols), lambda i, p: (0, jnp.where(i // per == p[0], i % per, 0), 0))
    far = pl.BlockSpec((1, tile, cols), lambda i, p: (0, jnp.where(i // per == p[0], 0, i % per), 0))
    row = lambda n: pl.BlockSpec((tile, n), lambda i, p: (i, 0))
    line = pl.BlockSpec((1, cols), lambda i, p: (0, 0))
    shape = lambda *s: jax.ShapeDtypeStruct(s, jnp.float32)
    return pl.pallas_call(
        functools.partial(finish_kernel, with_qkv=bool(extra), line_row=width % tile),
        grid_spec=pltpu.PrefetchScalarGridSpec(
            num_scalar_prefetch=1,
            grid=(2 * per,),
            in_specs=[own, far] + [row(a.shape[1]) for a in extra] + [anywhere],
            out_specs=[row(cols), line] + [row(1)] * (len(extra) // 2),
        ),
        out_shape=[shape(width, cols), shape(1, cols)] + [shape(width, 1)] * (len(extra) // 2),
        compiler_params=pltpu.CompilerParams(vmem_limit_bytes=vmem_bytes),
        cost_estimate=light,
        name="finish",
    )(place, own_rows, other_rows, *extra, earlier)


def layout(lengths, positions):
    segment = jnp.zeros_like(positions)
    begin = jnp.zeros_like(positions)
    end = jnp.int32(0)
    for n in range(lengths.shape[0]):
        end = end + lengths[n]
        later = positions >= end
        segment = segment + later.astype(jnp.int32)
        begin = jnp.where(later, end, begin)
    return (segment, positions - begin)


def swap(value, axis, bit):
    count = lax.axis_size(axis)
    return lax.ppermute(value, axis, [(i, i ^ bit) for i in range(count)])


def high_bits(count):
    bits, bit = [], 2
    while bit < count:
        bits.append(bit)
        bit *= 2
    return bits


def spread_far(value):
    blocks = {0: value}
    for bit in high_bits(lax.axis_size("mp")):
        for offset in sorted(blocks):
            blocks[offset | bit] = swap(blocks[offset], "mp", bit)
    return blocks


def wide(value):
    return value.astype(jnp.float32)


def wide(value):
    return value.astype(jnp.float32)


def last_pair(parts, earlier):
    parts = {o: parts[o] for o in parts if o % 2 == 0}
    bits = high_bits(lax.axis_size("mp"))
    for bit in bits[:-1]:
        parts = {o: total(parts[o][None], swap(parts[o | bit], "mp", bit)[None], earlier)[0] for o in parts if not o & bit}
    return parts[0], swap(parts[bits[-1]], "mp", bits[-1])


def copied(value, earlier):
    def kernel(value_ref, _, out_ref):
        out_ref[...] = value_ref[...]

    return call(kernel, [short(*value.shape)], [value], earlier, (), "copied")[0]


def all_bits(count):
    return [1] + high_bits(count) if count > 1 else []


def bit_of(axis, bit):
    return lax.rem(lax.axis_index(axis) // bit, 2)[None]


class Scatter:
    def __init__(self, parts):
        self.sent, self.kept = parts
        self.bits = all_bits(lax.axis_size("dp"))
        self.came = swap(self.sent, "dp", self.bits[0])

    def step(self, earlier):
        if not self.bits:
            return earlier
        self.bits = self.bits[1:]
        if not self.bits:
            self.result = total(self.kept, self.came, earlier, jnp.float32)[0]
            return self.result
        self.sent, self.kept = split(self.kept, self.came, bit_of("dp", self.bits[0]), earlier)
        self.came = swap(self.sent, "dp", self.bits[0])
        return self.kept


class Sum:
    def __init__(self, sent, kept):
        route = [("mp", b) for b in all_bits(lax.axis_size("mp"))] + [("dp", b) for b in all_bits(lax.axis_size("dp"))]
        self.down, self.up = route[1:], []
        self.kept = kept
        self.came = swap(sent, "mp", 1)

    def step(self, earlier):
        if self.done():
            return earlier
        if self.down is not None:
            while self.down:
                axis, bit = self.down.pop(0)
                rows = self.kept.shape[1] // 2
                if rows % 16:
                    self.kept = total(self.kept, self.came, earlier)
                    self.came = swap(self.kept, axis, bit)
                    return self.kept
                view = lambda v: v.reshape(2, rows, v.shape[2])
                self.up.append((axis, bit))
                sent, self.kept = split(view(self.kept), view(self.came), bit_of(axis, bit), earlier)
                self.came = swap(sent, axis, bit)
                return self.kept
            self.down = None
            self.kept = total(self.kept, self.came, earlier)
        else:
            axis, bit = self.up.pop()
            own = weave(self.kept, self.came, bit_of(axis, bit), earlier)
            self.kept = own.reshape(1, -1, own.shape[2])
        axis, bit = self.up[-1] if self.up else ("mp", 1)
        self.came = swap(self.kept, axis, bit)
        return self.kept

    def done(self):
        return self.down is None and not self.up


def on_device(
    tokens,
    seq_lengths,
    attn_gain,
    qkv_weight,
    qkv_bias,
    out_weight,
    mlp_gain,
    gate_weight,
    up_weight,
    down_weight,
    cotangent,
):
    tok_rows, width = tokens.shape
    mp_count = lax.axis_size("mp")
    mp_index = lax.axis_index("mp")
    q_rows = HEADS * HEAD
    lengths = seq_lengths[0]
    steps = jnp.arange(tok_rows, dtype=jnp.int32)
    segment, position = layout(lengths, mp_index * tok_rows + steps)
    key_rows = [(mp_index ^ o) * tok_rows + steps for o in range(mp_count)]
    key_segment, key_position = layout(lengths, jnp.concatenate(key_rows))
    bounds = jnp.stack([(mp_index * tok_rows - position[0]) // tok_rows, mp_index]).astype(jnp.int32)
    marks = jnp.arange(MARKS, dtype=jnp.int32)
    query_marks = (segment[None, :] != marks[:, None]).astype(jnp.bfloat16)
    key_marks = jnp.where(key_segment[:, None] == marks[None, :], masked_score, 0.0).astype(jnp.bfloat16)
    inverse_freq = rope_base ** (-2.0 * jnp.arange(HEAD // 2, dtype=jnp.float32) / HEAD)
    key_angles = inverse_freq[:, None] * key_position.astype(jnp.float32)[None, :]
    cos_keys, sin_keys = jnp.cos(key_angles), jnp.sin(key_angles)

    normed, queries, own_kv = project(tokens, attn_gain, qkv_weight, qkv_bias, cos_keys, sin_keys)
    blocks = spread_far(own_kv)
    blocks.update({o | 1: swap(blocks[o], "mp", 1) for o in sorted(blocks)})
    blocks = [blocks[o] for o in range(mp_count)]

    cot = copied(cotangent, blocks[2])
    cots = spread_far(cot)
    cots[1] = swap(cotangent, "mp", 1)
    attended, log_totals = attend(bounds, queries, query_marks, key_marks, blocks, cot)
    for o in range(2, mp_count, 2):
        cots[o | 1] = swap(cots[o], "mp", 1)

    middle, normed_mid = call(
        middle_kernel,
        [jax.ShapeDtypeStruct((tok_rows, width), jnp.float32), short(tok_rows, width)],
        [tokens, attended, out_weight, mlp_gain[None]],
        cot,
        name="middle",
    )
    gate_t, up_t = gate_weight.T, up_weight.T
    mids = {0: normed_mid, 1: swap(normed_mid, "mp", 1)}
    mids.update(spread_far(normed_mid))
    outs, grads, hids, ggs, gus = {}, {}, [], [], []
    clock = normed_mid
    for o in range(0, mp_count, 2):
        if o:
            mids[o] = after(mids[o], clock)
            mids[o | 1] = swap(mids[o], "mp", 1)
        pair = [o, o | 1]
        out, grad, hid, gg, gu = feed_forward(
            [mids[k] for k in pair], [cots[k] for k in pair], gate_t, up_t, down_weight, clock
        )
        clock = hid
        hids.append(hid), ggs.append(gg), gus.append(gu)
        for k in (0, 1):
            outs[o | k], grads[o | k] = out[k], grad[k]
    xs = [mids[o] for o in range(mp_count)]
    cs = [cots[o] for o in range(mp_count)]

    near_grads = add_pairs(grads, clock)
    clock = near_grads[0]
    dp_count = lax.axis_size("dp")
    low = bit_of("dp", 1)
    wide_down = weight_grad(cs, hids, low, 1, dp_count, clock)
    near_outs = add_pairs(outs, wide_down[0])
    wide_gate = weight_grad(xs, ggs, low, 1, dp_count, near_outs[0])
    wide_up = weight_grad(xs, gus, low, 1, dp_count, wide_gate[0])
    down_sum, gate_sum, up_sum = Scatter(wide_down), Scatter(wide_gate), Scatter(wide_up)
    clock = wide_up[0]
    near_outs = {o: after(near_outs[o], clock) if o else near_outs[o] for o in near_outs}
    outs = last_pair(near_outs, clock)
    core = bit_of("mp", 1)
    half = normed.shape[1] // 2
    grad_middle, grad_attended, *out_halves = call(
        branch_kernel,
        [jax.ShapeDtypeStruct((tok_rows, width), jnp.float32), short(q_rows, tok_rows), short(1, half, width), short(1, half, width)],
        [*last_pair(near_grads, clock), middle, mlp_gain[None], cotangent, out_weight, attended],
        clock,
        [core],
        "branch",
    )
    out_sum = Sum(*out_halves)
    clock = down_sum.step(grad_attended)
    back = functools.partial(
        attend_back,
        bounds=bounds,
        q=queries,
        query_marks=query_marks,
        key_marks=key_marks,
        o=attended,
        go=grad_attended,
        log=log_totals,
        cos_table=cos_keys,
        sin_table=sin_keys,
        blocks=blocks,
    )
    grad_qs, kv_pairs = [], []
    for head in range(KV_HEADS):
        grad_q, kv_even, kv_odd = back(head, earlier=clock)
        grad_qs.append(grad_q)
        kv_pairs += [kv_even, swap(kv_odd, "mp", 1)]
        clock = grad_q
        if head == 0:
            for item in (out_sum, gate_sum, down_sum):
                clock = item.step(clock)
            output = clock = call(output_kernel, [short(tok_rows, width)], [middle, *outs], clock, name="output")[0]
    near_kv = call(
        functools.partial(near_keys_kernel, heads=KV_HEADS),
        [short(KV_HEADS * 2 * HEAD, tok_rows)] * (mp_count // 2),
        kv_pairs,
        clock,
        name="near_keys",
    )
    kv_sums = last_pair({2 * n: a for n, a in enumerate(near_kv)}, near_kv[0])
    clock = near_kv[0]
    for item in (out_sum, up_sum, gate_sum, down_sum):
        clock = item.step(clock)
    grad_keys, grad_values = call(merge_kernel, [short(KV_HEADS * HEAD, tok_rows)] * 2, kv_sums, clock, name="merge")
    rows = [*grad_qs, grad_keys, grad_values]
    sent = outer(1 - core, normed, rows, grad_keys)
    kept = outer(core, normed, rows, sent)
    qkv_sum = Sum(sent, kept)

    clock = out_sum.step(kept)
    clock = qkv_sum.step(clock)
    grad_tokens = clock = call(
        functools.partial(tokens_kernel, count=len(rows)),
        [jax.ShapeDtypeStruct((tok_rows, width), jnp.float32)],
        [*rows, qkv_weight, tokens, attn_gain[None], grad_middle],
        clock,
        name="tokens",
        scratch=[pltpu.VMEM((qkv_weight.shape[1], tok_rows), jnp.bfloat16)],
    )[0]
    for item in (up_sum, out_sum, gate_sum, out_sum, qkv_sum, qkv_sum, out_sum, up_sum):
        clock = item.step(clock)
    for item in (down_sum, gate_sum, up_sum) * 8:
        clock = item.step(clock)
    while not out_sum.done():
        clock = out_sum.step(qkv_sum.step(clock))
    grad_out_weight, gain_line = finish(core, out_sum.kept, out_sum.came, width, clock)
    clock = gain_line
    while not qkv_sum.done():
        clock = qkv_sum.step(clock)
    grad_qkv_weight, bias_line, grad_attn_gain = finish(
        core, qkv_sum.kept, qkv_sum.came, width, clock, [qkv_weight, wide(attn_gain)[:, None]]
    )

    return (
        output,
        grad_tokens,
        grad_attn_gain[:, 0],
        grad_qkv_weight,
        bias_line[0],
        grad_out_weight,
        gain_line[0],
        gate_sum.result,
        up_sum.result,
        down_sum.result.T,
    )


def solution(mesh):
    return jax.shard_map(
        on_device,
        mesh=mesh,
        in_specs=(
            P(("dp", "mp"), None),
            P("dp", None),
            P(),
            P(),
            P(),
            P(),
            P(),
            P(None, "mp"),
            P(None, "mp"),
            P("mp", None),
            P(("dp", "mp"), None),
        ),
        out_specs=(
            P(("dp", "mp"), None),
            P(("dp", "mp"), None),
            P(),
            P(),
            P(),
            P(),
            P(),
            P("dp", "mp"),
            P("dp", "mp"),
            P("mp", "dp"),
        ),
        check_vma=False,
    )
```

```python
import functools

import jax
import jax.numpy as jnp
from jax import lax
from jax.experimental import pallas as pl
from jax.experimental.pallas import tpu as pltpu
from jax.sharding import PartitionSpec as P

HEADS = 14
KV_HEADS = 2
HEAD = 64
MARKS = 16

norm_epsilon = 1e-06
rope_base = 1000000.0
masked_score = -1e30
vmem_bytes = 52 * 2**20


anywhere = pl.BlockSpec(memory_space=pltpu.HBM)
light = pl.CostEstimate(flops=1000, bytes_accessed=1000, transcendentals=0)


def dot(left, right, left_dim, right_dim):
    return lax.dot_general(
        left, right, (((left_dim,), (right_dim,)), ((), ())), preferred_element_type=jnp.float32
    )


def causal(tile):
    key_id = lax.broadcasted_iota(jnp.int32, tile.shape, 0)
    query_id = lax.broadcasted_iota(jnp.int32, tile.shape, 1)
    return jnp.where(key_id <= query_id, tile, masked_score)


def turn(values, cos_table, sin_table):
    half = HEAD // 2
    pieces = []
    for row in range(0, values.shape[0], HEAD):
        lower, upper = values[row : row + half], values[row + half : row + HEAD]
        pieces += [lower * cos_table - upper * sin_table, upper * cos_table + lower * sin_table]
    return pieces


def project_kernel(tok_ref, gain_ref, weight_ref, bias_ref, cos_ref, sin_ref, normed_ref, q_ref, kv_ref):
    values = tok_ref[...].astype(jnp.float32)
    inverse = lax.rsqrt(jnp.mean(values * values, axis=-1, keepdims=True) + norm_epsilon)
    normed = (values * inverse * gain_ref[...].astype(jnp.float32)).astype(jnp.bfloat16)
    rows, width = normed.shape
    normed_ref[:, 0:width] = normed
    ones_at = lax.broadcasted_iota(jnp.int32, (rows, normed_ref.shape[1] - width), 1) == 0
    normed_ref[:, width:] = jnp.where(ones_at, 1.0, 0.0).astype(jnp.bfloat16)
    cos_table, sin_table = cos_ref[:, 0:rows], sin_ref[:, 0:rows]
    q_width, kv_width, half = HEADS * HEAD, KV_HEADS * HEAD, HEAD // 2
    step = 128
    for lo in range(0, weight_ref.shape[1], step):
        cols = slice(lo, lo + step)
        part = dot(normed, weight_ref[:, cols], 1, 0) + bias_ref[:, cols].astype(jnp.float32)
        part = part.T
        if lo < q_width + kv_width:
            pieces = turn(part, cos_table, sin_table)
        else:
            pieces = [part[r : r + half] for r in range(0, step, half)]
        for n, piece in enumerate(pieces):
            row = lo + n * half
            piece = piece.astype(jnp.bfloat16)
            if row < q_width:
                q_ref[row : row + half, :] = piece * jnp.bfloat16(HEAD ** (-0.5))
            else:
                row -= q_width
                which, row = row // kv_width, row % kv_width
                head, row = row // HEAD, row % HEAD
                place = (2 * head + which) * HEAD + row
                kv_ref[place : place + half, :] = piece


def project(tokens, gain, weight, bias, cos_table, sin_table):
    rows, width = tokens.shape
    shape = lambda *s: jax.ShapeDtypeStruct(s, jnp.bfloat16)
    return pl.pallas_call(
        project_kernel,
        out_shape=[shape(rows, width + 128), shape(HEADS * HEAD, rows), shape(2 * KV_HEADS * HEAD, rows)],
        compiler_params=pltpu.CompilerParams(vmem_limit_bytes=vmem_bytes),
        cost_estimate=light,
        name="project",
    )(tokens, gain[None], weight, bias[None], cos_table, sin_table)


def load_keys(blocks, marks_ref, kx, vx, vk):
    rows = blocks[0].shape[1]
    for o, block in enumerate(blocks):
        spot = slice(o * rows, (o + 1) * rows)
        flat = block[...].astype(jnp.float32).T.astype(jnp.bfloat16)
        kx[spot, 0:HEAD] = flat[:, 0:HEAD]
        if vk is not None:
            vk[spot, :] = flat[:, HEAD:]
        if vx is not None:
            vx[0:HEAD, spot] = block[HEAD:, :]
    kx[:, HEAD:] = marks_ref[...]
    if vx is not None:
        vx[HEAD:, :] = jnp.ones((MARKS, vx.shape[1]), jnp.bfloat16)


def staged(items, begin, finish):
    earlier = None
    for item in items:
        state = begin(item)
        if earlier is not None:
            finish(*earlier)
        earlier = (item, state)
    finish(*earlier)


def attend_kernel(bounds, q_ref, mark_ref, marks_ref, *refs, count):
    blocks = refs[:count]
    out_ref, log_ref, kx, vx, q_ext, acc, top = refs[-7:]
    rows = q_ref.shape[1]
    half = rows // 2
    heads = q_ref.shape[0] // HEAD
    load_keys(blocks, marks_ref, kx, vx, None)
    for h in range(heads):
        q_ext[h, 0:HEAD, :] = q_ref[h * HEAD : (h + 1) * HEAD, :]
        q_ext[h, HEAD:, :] = mark_ref[...]
    acc[...] = jnp.zeros_like(acc)
    top[...] = jnp.full_like(top, 2 * masked_score)

    def begin(item):
        h, start, size, lo, hi, diag = item
        scores = dot(kx[pl.ds(start, size), :], q_ext[h, :, lo:hi], 1, 0)
        return causal(scores) if diag else scores

    def finish(item, scores):
        h, start, size, lo, hi, diag = item
        old = top[h, :, lo:hi]
        new = jnp.maximum(old, jnp.max(scores, axis=0, keepdims=True))
        weights = jnp.exp(scores - new).astype(jnp.bfloat16)
        top[h, :, lo:hi] = new
        acc[h, :, lo:hi] = acc[h, :, lo:hi] * jnp.exp(old - new) + dot(vx[:, pl.ds(start, size)], weights, 1, 0)

    first, own = bounds[0], bounds[1]

    for o in range(1, count):
        c = own ^ o

        @pl.when((c >= first) & (c < own))
        def _():
            staged([(h, o * rows, rows, 0, rows, False) for h in range(heads)], begin, finish)

    spots = [(0, half, half, rows, False), (0, half, 0, half, True), (half, half, half, rows, True)]
    staged([(h,) + spot for h in range(heads) for spot in spots], begin, finish)
    for h in range(heads):
        total = acc[h, HEAD : HEAD + 1, :]
        out_ref[h * HEAD : (h + 1) * HEAD, :] = (acc[h, 0:HEAD, :] / total).astype(jnp.bfloat16)
        log_ref[h] = top[h] + jnp.log(total)


def attend(bounds, q, query_marks, key_marks, blocks, earlier):
    width, rows = q.shape
    heads = width // HEAD
    rep = heads // KV_HEADS
    group = key_marks.shape[0]
    whole = lambda a: pl.BlockSpec(a.shape, lambda g, b: (0, 0))
    by_head = lambda n: pl.BlockSpec((n, rows), lambda g, b: (g, 0))
    return pl.pallas_call(
        functools.partial(attend_kernel, count=len(blocks)),
        grid_spec=pltpu.PrefetchScalarGridSpec(
            num_scalar_prefetch=1,
            grid=(KV_HEADS,),
            in_specs=[by_head(rep * HEAD), whole(query_marks), whole(key_marks)] + [by_head(2 * HEAD)] * len(blocks) + [anywhere],
            out_specs=[by_head(rep * HEAD), pl.BlockSpec((rep, 1, rows), lambda g, b: (g, 0, 0))],
            scratch_shapes=[
                pltpu.VMEM((group, HEAD + MARKS), jnp.bfloat16),
                pltpu.VMEM((HEAD + MARKS, group), jnp.bfloat16),
                pltpu.VMEM((rep, HEAD + MARKS, rows), jnp.bfloat16),
                pltpu.VMEM((rep, HEAD + MARKS, rows), jnp.float32),
                pltpu.VMEM((rep, 1, rows), jnp.float32),
            ],
        ),
        out_shape=[
            jax.ShapeDtypeStruct((width, rows), jnp.bfloat16),
            jax.ShapeDtypeStruct((heads, 1, rows), jnp.float32),
        ],
        compiler_params=pltpu.CompilerParams(vmem_limit_bytes=vmem_bytes),
        cost_estimate=light,
        name="attend",
    )(bounds, q, query_marks, key_marks, *blocks, earlier)


def attend_back_kernel(
    bounds, q_ref, mark_ref, marks_ref, o_ref, go_ref, log_ref, cos_ref, sin_ref, *refs, count
):
    blocks = refs[:count]
    refs = refs[count + 1 :]
    gq_ref = refs[0]
    gkv_refs = refs[1:3]
    kx, vk, q_ext, acc, delta, gkv = refs[3:]
    rows = q_ref.shape[1]
    half = rows // 2
    heads = q_ref.shape[0] // HEAD
    load_keys(blocks, marks_ref, kx, None, vk)
    for h in range(heads):
        spot = slice(h * HEAD, (h + 1) * HEAD)
        q_ext[h, 0:HEAD, :] = q_ref[spot, :]
        q_ext[h, HEAD:, :] = mark_ref[...]
        product = o_ref[spot, :].astype(jnp.float32) * go_ref[spot, :].astype(jnp.float32)
        delta[h] = jnp.sum(product, axis=0, keepdims=True)
    acc[...] = jnp.zeros_like(acc)
    gkv[...] = jnp.zeros_like(gkv)

    def begin(item):
        h, start, size, lo, hi, diag, keys_t = item
        scores = dot(kx[pl.ds(start, size), :], q_ext[h, :, lo:hi], 1, 0)
        grad_prob = dot(vk[pl.ds(start, size), :], go_ref[h * HEAD : (h + 1) * HEAD, lo:hi], 1, 0)
        return (causal(scores) if diag else scores), grad_prob

    def finish(item, state):
        h, start, size, lo, hi, diag, keys_t = item
        scores, grad_prob = state
        spot = slice(h * HEAD, (h + 1) * HEAD)
        prob = jnp.exp(scores - log_ref[h, :, lo:hi])
        grad_score = (prob * (grad_prob - delta[h, :, lo:hi])).astype(jnp.bfloat16)
        gkv[HEAD:, pl.ds(start, size)] += dot(go_ref[spot, lo:hi], prob.astype(jnp.bfloat16), 1, 1)
        gkv[0:HEAD, pl.ds(start, size)] += dot(q_ref[spot, lo:hi], grad_score, 1, 1)
        acc[h, :, lo:hi] += dot(keys_t, grad_score, 1, 0)

    first, own = bounds[0], bounds[1]
    for o in range(1, count):
        c = own ^ o

        @pl.when((c >= first) & (c < own))
        def _():
            keys_t = blocks[o][0:HEAD, :]
            staged([(h, o * rows, rows, 0, rows, False, keys_t) for h in range(heads)], begin, finish)

    low, high = blocks[0][0:HEAD, 0:half], blocks[0][0:HEAD, half:]
    spots = [(0, half, half, rows, False, low), (0, half, 0, half, True, low), (half, half, half, rows, True, high)]
    staged([(h,) + spot for h in range(heads) for spot in spots], begin, finish)
    cos_own, sin_own = cos_ref[:, 0:rows], -sin_ref[:, 0:rows]
    for h in range(heads):
        pieces = turn(acc[h] * (HEAD ** (-0.5)), cos_own, sin_own)
        for n, piece in enumerate(pieces):
            row = h * HEAD + n * (HEAD // 2)
            gq_ref[row : row + HEAD // 2, :] = piece.astype(jnp.bfloat16)
    for o in range(count):
        spot = slice(o * rows, (o + 1) * rows)
        pieces = turn(gkv[0:HEAD, spot], cos_ref[:, spot], -sin_ref[:, spot])
        for n, piece in enumerate(pieces):
            gkv_refs[o % 2][o // 2, n * (HEAD // 2) : (n + 1) * (HEAD // 2), :] = piece.astype(jnp.bfloat16)
        gkv_refs[o % 2][o // 2, HEAD:, :] = gkv[HEAD:, spot].astype(jnp.bfloat16)


def attend_back(head, bounds, q, query_marks, key_marks, o, go, log, cos_table, sin_table, blocks, earlier):
    width, rows = q.shape
    rep = HEADS // KV_HEADS
    group = key_marks.shape[0]
    count = len(blocks)
    whole = lambda a: pl.BlockSpec(a.shape, lambda i, b: (0, 0))
    by_head = lambda n: pl.BlockSpec((n, rows), lambda i, b: (head, 0))
    return pl.pallas_call(
        functools.partial(attend_back_kernel, count=count),
        grid_spec=pltpu.PrefetchScalarGridSpec(
            num_scalar_prefetch=1,
            grid=(1,),
            in_specs=[by_head(rep * HEAD), whole(query_marks), whole(key_marks), by_head(rep * HEAD), by_head(rep * HEAD)]
            + [pl.BlockSpec((rep, 1, rows), lambda i, b: (head, 0, 0)), whole(cos_table), whole(sin_table)]
            + [by_head(2 * HEAD)] * count
            + [anywhere],
            out_specs=[pl.BlockSpec((rep * HEAD, rows), lambda i, b: (0, 0))]
            + [pl.BlockSpec((count // 2, 2 * HEAD, rows), lambda i, b: (0, 0, 0))] * 2,
            scratch_shapes=[
                pltpu.VMEM((group, HEAD + MARKS), jnp.bfloat16),
                pltpu.VMEM((group, HEAD), jnp.bfloat16),
                pltpu.VMEM((rep, HEAD + MARKS, rows), jnp.bfloat16),
                pltpu.VMEM((rep, HEAD, rows), jnp.float32),
                pltpu.VMEM((rep, 1, rows), jnp.float32),
                pltpu.VMEM((2 * HEAD, group), jnp.float32),
            ],
        ),
        out_shape=[jax.ShapeDtypeStruct((rep * HEAD, rows), jnp.bfloat16)]
        + [jax.ShapeDtypeStruct((count // 2, 2 * HEAD, rows), jnp.bfloat16)] * 2,
        compiler_params=pltpu.CompilerParams(vmem_limit_bytes=vmem_bytes),
        cost_estimate=light,
        name="attend_back",
    )(bounds, q, query_marks, key_marks, o, go, log, cos_table, sin_table, *blocks, earlier)


def act_kernel(*refs, count, steps):
    xs, cots = refs[:count], refs[count : 2 * count]
    gate_ref, up_ref, down_ref = refs[2 * count : 2 * count + 3]
    refs = refs[2 * count + 4 :]
    outs, grads = refs[:count], refs[count : 2 * count]
    hid_ref, gg_ref, gu_ref = refs[2 * count :]
    i = pl.program_id(0)

    def run(n):
        x = xs[n][...]
        gate = dot(x, gate_ref[...], 1, 1)
        up = dot(x, up_ref[...], 1, 1)
        grad_hidden = dot(cots[n][...], down_ref[...], 1, 1)
        sig = jax.nn.sigmoid(gate)
        silu = gate * sig
        hidden = (silu * up).astype(jnp.bfloat16)
        grad_gate = (grad_hidden * up * (sig * (1.0 + gate * (1.0 - sig)))).astype(jnp.bfloat16)
        grad_up = (grad_hidden * silu).astype(jnp.bfloat16)
        hid_ref[...] = hidden
        gg_ref[...] = grad_gate
        gu_ref[...] = grad_up
        grads[n][...] = (dot(grad_gate, gate_ref[...], 1, 0) + dot(grad_up, up_ref[...], 1, 0)).astype(jnp.bfloat16)
        outs[n][...] = dot(hidden, down_ref[...], 1, 0).astype(jnp.bfloat16)

    for n in range(count):
        pl.when(i // steps == n)(functools.partial(run, n))


def feed_forward(xs, cots, gate_t, up_t, down_weight, earlier):
    rows, width = xs[0].shape
    units = gate_t.shape[0]
    count = len(xs)
    tile = min(256, rows)
    steps = rows // tile

    def chunk(n):
        return pl.BlockSpec((tile, width), lambda i: (jnp.clip(i - n * steps, 0, steps - 1), 0))

    whole = lambda w: pl.BlockSpec(w.shape, lambda i: (0, 0), pipeline_mode=pl.Buffered(1))
    by_rows = pl.BlockSpec((tile, units), lambda i: (i, 0))
    small = jax.ShapeDtypeStruct((rows, width), jnp.bfloat16)
    large = jax.ShapeDtypeStruct((count * rows, units), jnp.bfloat16)
    result = pl.pallas_call(
        functools.partial(act_kernel, count=count, steps=steps),
        grid=(count * steps,),
        in_specs=[chunk(n) for n in range(count)] * 2 + [whole(gate_t), whole(up_t), whole(down_weight), anywhere],
        out_specs=[chunk(n) for n in range(count)] * 2 + [by_rows] * 3,
        out_shape=[small] * (2 * count) + [large] * 3,
        compiler_params=pltpu.CompilerParams(vmem_limit_bytes=vmem_bytes),
        cost_estimate=light,
        name="feed_forward",
    )(*xs, *cots, gate_t, up_t, down_weight, earlier)
    return result[:count], result[count : 2 * count], *result[2 * count :]


def weight_kernel(place, *refs, count, groups, bit):
    lefts, rights = refs[:count], refs[count : count + groups]
    sent_ref, kept_ref, acc = refs[-3:]
    i = pl.program_id(0)

    for n in range(count):

        @pl.when(i == n)
        def _():
            product = dot(lefts[n][...], rights[n * groups // count][...], 0, 0)
            acc[...] = product if n == 0 else acc[...] + product

    @pl.when(i == count - 1)
    def _():
        pieces, rows, _ = sent_ref.shape
        for ref, which in ((sent_ref, 1 - place[0]), (kept_ref, place[0])):
            for n in range(pieces):
                low, high = n % bit, n // bit
                start = (high * 2 * bit + low) * rows
                if rows % 16 == 0:
                    block = acc[pl.ds(pl.multiple_of(start + which * bit * rows, rows), rows), :]
                else:
                    upper = start + bit * rows
                    block = jnp.where(which == 0, acc[start : start + rows, :], acc[upper : upper + rows, :])
                ref[n] = block.astype(jnp.bfloat16)


def weight_grad(lefts, rights, place, bit, dp_count, earlier):
    rows, width = lefts[0].shape
    units = rights[0].shape[1]
    count, groups = len(lefts), len(rights)
    per = count // groups

    def part(g):
        return pl.BlockSpec((rows, units), lambda i, p: (jnp.clip(i - g * per, 0, per - 1), 0))

    pieces = dp_count // 2
    out_spec = pl.BlockSpec((pieces, width // dp_count, units), lambda i, p: (0, 0, 0), pipeline_mode=pl.Buffered(1))
    return pl.pallas_call(
        functools.partial(weight_kernel, count=count, groups=groups, bit=bit),
        grid_spec=pltpu.PrefetchScalarGridSpec(
            num_scalar_prefetch=1,
            grid=(count,),
            in_specs=[pl.BlockSpec((rows, width), lambda i, p: (0, 0))] * count
            + [part(g) for g in range(groups)]
            + [anywhere],
            out_specs=[out_spec] * 2,
            scratch_shapes=[pltpu.VMEM((width, units), jnp.float32)],
        ),
        out_shape=[jax.ShapeDtypeStruct((pieces, width // dp_count, units), jnp.bfloat16)] * 2,
        compiler_params=pltpu.CompilerParams(vmem_limit_bytes=vmem_bytes),
        cost_estimate=light,
        name="weight_grad",
    )(place, *lefts, *rights, earlier)


def order_kernel(value_ref, earlier_ref, out_ref):
    pass


def after(value, earlier):
    return pl.pallas_call(
        order_kernel,
        in_specs=[anywhere] * 2,
        out_specs=anywhere,
        out_shape=jax.ShapeDtypeStruct(value.shape, value.dtype),
        input_output_aliases={0: 0},
        name="after",
    )(value, earlier)


def call(kernel, outs, args, earlier, places=(), name=None, scratch=()):
    whole = lambda shape: pl.BlockSpec(shape, lambda i, *p: (0,) * len(shape))
    result = pl.pallas_call(
        kernel,
        grid_spec=pltpu.PrefetchScalarGridSpec(
            num_scalar_prefetch=len(places),
            grid=(1,),
            in_specs=[whole(a.shape) for a in args] + [anywhere],
            out_specs=[whole(o.shape) for o in outs],
            scratch_shapes=scratch,
        ),
        out_shape=outs,
        compiler_params=pltpu.CompilerParams(vmem_limit_bytes=vmem_bytes),
        cost_estimate=light,
        name=name,
    )(*places, *args, earlier)
    return result


def short(*shape):
    return jax.ShapeDtypeStruct(shape, jnp.bfloat16)


def added(first_ref, second_ref, n):
    return first_ref[n].astype(jnp.float32) + second_ref[n].astype(jnp.float32)


def split_kernel(place, kept_ref, came_ref, _, sent_out, kept_out):
    for n in range(sent_out.shape[0]):
        for out, which in ((sent_out, 1 - place[0]), (kept_out, place[0])):
            out[n] = added(kept_ref, came_ref, 2 * n + which).astype(out.dtype)


def split(kept, came, place, earlier):
    half = (kept.shape[0] // 2,) + kept.shape[1:]
    return call(split_kernel, [short(*half)] * 2, [kept, came], earlier, [place], "split")


def total_kernel(kept_ref, came_ref, _, out_ref):
    for n in range(out_ref.shape[0]):
        out_ref[n] = added(kept_ref, came_ref, n).astype(out_ref.dtype)


def total(kept, came, earlier, dtype=jnp.bfloat16):
    return call(total_kernel, [jax.ShapeDtypeStruct(kept.shape, dtype)], [kept, came], earlier, (), "total")[0]


def weave_kernel(place, own_ref, came_ref, _, out_ref):
    out_ref[place[0]] = own_ref[0]
    out_ref[1 - place[0]] = came_ref[0]


def weave(own, came, place, earlier):
    return call(weave_kernel, [short(2, *own.shape[1:])], [own, came], earlier, [place], "weave")[0]


def near_kernel(*refs, count):
    ins, outs = refs[: 2 * count], refs[2 * count + 1 :]
    for n in range(count):
        outs[n][...] = (ins[2 * n][...].astype(jnp.float32) + ins[2 * n + 1][...].astype(jnp.float32)).astype(outs[n].dtype)


def add_pairs(parts, earlier):
    evens = [o for o in sorted(parts) if o % 2 == 0]
    args = []
    for o in evens:
        args += [parts[o], swap(parts[o | 1], "mp", 1)]
    outs = [short(*parts[o].shape) for o in evens]
    result = call(functools.partial(near_kernel, count=len(evens)), outs, args, earlier, (), "add_pairs")
    return dict(zip(evens, result))


def middle_kernel(tok_ref, att_ref, weight_ref, gain_ref, _, mid_ref, normed_ref):
    middle = tok_ref[...].astype(jnp.float32) + dot(att_ref[...], weight_ref[...], 0, 0)
    inverse = lax.rsqrt(jnp.mean(middle * middle, axis=-1, keepdims=True) + norm_epsilon)
    mid_ref[...] = middle
    normed_ref[...] = (middle * inverse * gain_ref[...].astype(jnp.float32)).astype(jnp.bfloat16)


def norm_back(values, gain, grad_out):
    inverse = lax.rsqrt(jnp.mean(values * values, axis=-1, keepdims=True) + norm_epsilon)
    scaled = grad_out * gain
    mean_dot = jnp.mean(values * scaled, axis=-1, keepdims=True)
    return inverse * scaled - values * inverse * inverse * inverse * mean_dot, inverse


def branch_kernel(
    place, near_ref, came_ref, mid_ref, gain_ref, cot_ref, weight_ref, att_ref, _, grad_ref, branch_ref, sent_ref, kept_ref
):
    incoming = near_ref[...].astype(jnp.float32) + came_ref[...].astype(jnp.float32)
    middle = mid_ref[...]
    grad_mid, inverse = norm_back(middle, gain_ref[...].astype(jnp.float32), incoming)
    gain = jnp.sum(incoming * middle * inverse, axis=0, keepdims=True)
    grad_mid = cot_ref[...].astype(jnp.float32) + grad_mid
    grad_ref[...] = grad_mid
    branch = grad_mid.astype(jnp.bfloat16)
    branch_ref[...] = dot(weight_ref[...], branch, 1, 1).astype(jnp.bfloat16)
    half = sent_ref.shape[1]
    rest = att_ref.shape[0] - half
    for ref, which in ((sent_ref, 1 - place[0]), (kept_ref, place[0])):

        @pl.when(which == 0)
        def _():
            ref[0] = dot(att_ref[0:half, :], branch, 1, 0).astype(ref.dtype)

        @pl.when(which == 1)
        def _():
            ref[0, 0:rest, :] = dot(att_ref[half:, :], branch, 1, 0).astype(ref.dtype)
            line = lax.broadcasted_iota(jnp.int32, (half - rest, ref.shape[2]), 0) == 0
            ref[0, rest:, :] = jnp.where(line, gain, 0.0).astype(ref.dtype)


def output_kernel(mid_ref, near_ref, came_ref, _, out_ref):
    mlp = near_ref[...].astype(jnp.float32) + came_ref[...].astype(jnp.float32)
    out_ref[...] = (mid_ref[...] + mlp).astype(jnp.bfloat16)


def tokens_kernel(*refs, count):
    weight_ref, tok_ref, gain_ref, grad_ref, _, out_ref, rows = refs[count:]
    at = 0
    for ref in refs[:count]:
        rows[at : at + ref.shape[0], :] = ref[...]
        at += ref.shape[0]
    grad_normed = dot(rows[...], weight_ref[...], 0, 1)
    grad_in, _ = norm_back(tok_ref[...].astype(jnp.float32), gain_ref[...].astype(jnp.float32), grad_normed)
    out_ref[...] = grad_ref[...] + grad_in


def outer_kernel(place, left_ref, *refs):
    rights, out_ref = refs[:-2], refs[-1]
    half = out_ref.shape[1]
    left = left_ref[:, pl.ds(pl.multiple_of(place[0] * half, 128), half)]
    at = 0
    for ref in rights:
        out_ref[0, :, at : at + ref.shape[0]] = dot(left, ref[...], 0, 1).astype(out_ref.dtype)
        at += ref.shape[0]


def outer(place, left, rights, earlier):
    shape = short(1, left.shape[1] // 2, sum(r.shape[0] for r in rights))
    return call(outer_kernel, [shape], [left, *rights], earlier, [place], "outer")[0]


def near_keys_kernel(*refs, heads):
    ins, outs = refs[: 2 * heads], refs[2 * heads + 1 :]
    for h in range(heads):
        for n, out in enumerate(outs):
            both = added(ins[2 * h], ins[2 * h + 1], n)
            out[h * 2 * HEAD : (h + 1) * 2 * HEAD, :] = both.astype(jnp.bfloat16)


def merge_kernel(first_ref, second_ref, _, keys_out, values_out):
    both = (first_ref[...].astype(jnp.float32) + second_ref[...].astype(jnp.float32)).astype(jnp.bfloat16)
    for h in range(keys_out.shape[0] // HEAD):
        spot = slice(h * HEAD, (h + 1) * HEAD)
        keys_out[spot, :] = both[2 * h * HEAD : (2 * h + 1) * HEAD]
        values_out[spot, :] = both[(2 * h + 1) * HEAD : (2 * h + 2) * HEAD]


def finish_kernel(place, own_ref, other_ref, *refs, with_qkv, line_row):
    i = pl.program_id(0)
    steps = pl.num_programs(0)
    mine = (i * 2 // steps) == place[0]
    sums = jnp.where(mine, own_ref[0], other_ref[0]).astype(jnp.float32)
    if with_qkv:
        weight_ref, gain_ref, _, out_ref, line_ref, again_ref = refs
    else:
        _, out_ref, line_ref = refs

    out_ref[...] = sums
    if with_qkv:
        product = sums * weight_ref[...].astype(jnp.float32)
        again_ref[...] = jnp.sum(product, axis=1, keepdims=True) / gain_ref[...]

    @pl.when(i == steps - 1)
    def _():
        line_ref[...] = sums[line_row : line_row + 1]


def finish(place, own_rows, other_rows, width, earlier, extra=()):
    _, half, cols = own_rows.shape
    tile = min(256, half)
    per = half // tile
    own = pl.BlockSpec((1, tile, cols), lambda i, p: (0, jnp.where(i // per == p[0], i % per, 0), 0))
    far = pl.BlockSpec((1, tile, cols), lambda i, p: (0, jnp.where(i // per == p[0], 0, i % per), 0))
    row = lambda n: pl.BlockSpec((tile, n), lambda i, p: (i, 0))
    line = pl.BlockSpec((1, cols), lambda i, p: (0, 0))
    shape = lambda *s: jax.ShapeDtypeStruct(s, jnp.float32)
    return pl.pallas_call(
        functools.partial(finish_kernel, with_qkv=bool(extra), line_row=width % tile),
        grid_spec=pltpu.PrefetchScalarGridSpec(
            num_scalar_prefetch=1,
            grid=(2 * per,),
            in_specs=[own, far] + [row(a.shape[1]) for a in extra] + [anywhere],
            out_specs=[row(cols), line] + [row(1)] * (len(extra) // 2),
        ),
        out_shape=[shape(width, cols), shape(1, cols)] + [shape(width, 1)] * (len(extra) // 2),
        compiler_params=pltpu.CompilerParams(vmem_limit_bytes=vmem_bytes),
        cost_estimate=light,
        name="finish",
    )(place, own_rows, other_rows, *extra, earlier)


def layout(lengths, positions):
    segment = jnp.zeros_like(positions)
    begin = jnp.zeros_like(positions)
    end = jnp.int32(0)
    for n in range(lengths.shape[0]):
        end = end + lengths[n]
        later = positions >= end
        segment = segment + later.astype(jnp.int32)
        begin = jnp.where(later, end, begin)
    return (segment, positions - begin)


def swap(value, axis, bit):
    count = lax.axis_size(axis)
    return lax.ppermute(value, axis, [(i, i ^ bit) for i in range(count)])


def high_bits(count):
    bits, bit = [], 2
    while bit < count:
        bits.append(bit)
        bit *= 2
    return bits


def spread_far(value):
    blocks = {0: value}
    for bit in high_bits(lax.axis_size("mp")):
        for offset in sorted(blocks):
            blocks[offset | bit] = swap(blocks[offset], "mp", bit)
    return blocks


def wide(value):
    return value.astype(jnp.float32)


def wide(value):
    return value.astype(jnp.float32)


def last_pair(parts, earlier):
    parts = {o: parts[o] for o in parts if o % 2 == 0}
    bits = high_bits(lax.axis_size("mp"))
    for bit in bits[:-1]:
        parts = {o: total(parts[o][None], swap(parts[o | bit], "mp", bit)[None], earlier)[0] for o in parts if not o & bit}
    return parts[0], swap(parts[bits[-1]], "mp", bits[-1])


def copied(value, earlier):
    def kernel(value_ref, _, out_ref):
        out_ref[...] = value_ref[...]

    return call(kernel, [short(*value.shape)], [value], earlier, (), "copied")[0]


def all_bits(count):
    return [1] + high_bits(count) if count > 1 else []


def bit_of(axis, bit):
    return lax.rem(lax.axis_index(axis) // bit, 2)[None]


class Scatter:
    def __init__(self, parts):
        self.sent, self.kept = parts
        self.bits = all_bits(lax.axis_size("dp"))
        self.came = swap(self.sent, "dp", self.bits[0])

    def step(self, earlier):
        if not self.bits:
            return earlier
        self.bits = self.bits[1:]
        if not self.bits:
            self.result = total(self.kept, self.came, earlier, jnp.float32)[0]
            return self.result
        self.sent, self.kept = split(self.kept, self.came, bit_of("dp", self.bits[0]), earlier)
        self.came = swap(self.sent, "dp", self.bits[0])
        return self.kept


class Sum:
    def __init__(self, sent, kept):
        route = [("mp", b) for b in all_bits(lax.axis_size("mp"))] + [("dp", b) for b in all_bits(lax.axis_size("dp"))]
        self.down, self.up = route[1:], []
        self.kept = kept
        self.came = swap(sent, "mp", 1)

    def step(self, earlier):
        if self.done():
            return earlier
        if self.down is not None:
            while self.down:
                axis, bit = self.down.pop(0)
                rows = self.kept.shape[1] // 2
                if rows % 16:
                    self.kept = total(self.kept, self.came, earlier)
                    self.came = swap(self.kept, axis, bit)
                    return self.kept
                view = lambda v: v.reshape(2, rows, v.shape[2])
                self.up.append((axis, bit))
                sent, self.kept = split(view(self.kept), view(self.came), bit_of(axis, bit), earlier)
                self.came = swap(sent, axis, bit)
                return self.kept
            self.down = None
            self.kept = total(self.kept, self.came, earlier)
        else:
            axis, bit = self.up.pop()
            own = weave(self.kept, self.came, bit_of(axis, bit), earlier)
            self.kept = own.reshape(1, -1, own.shape[2])
        axis, bit = self.up[-1] if self.up else ("mp", 1)
        self.came = swap(self.kept, axis, bit)
        return self.kept

    def done(self):
        return self.down is None and not self.up


def on_device(
    tokens,
    seq_lengths,
    attn_gain,
    qkv_weight,
    qkv_bias,
    out_weight,
    mlp_gain,
    gate_weight,
    up_weight,
    down_weight,
    cotangent,
):
    tok_rows, width = tokens.shape
    mp_count = lax.axis_size("mp")
    mp_index = lax.axis_index("mp")
    q_rows = HEADS * HEAD
    lengths = seq_lengths[0]
    steps = jnp.arange(tok_rows, dtype=jnp.int32)
    segment, position = layout(lengths, mp_index * tok_rows + steps)
    key_rows = [(mp_index ^ o) * tok_rows + steps for o in range(mp_count)]
    key_segment, key_position = layout(lengths, jnp.concatenate(key_rows))
    bounds = jnp.stack([(mp_index * tok_rows - position[0]) // tok_rows, mp_index]).astype(jnp.int32)
    marks = jnp.arange(MARKS, dtype=jnp.int32)
    query_marks = (segment[None, :] != marks[:, None]).astype(jnp.bfloat16)
    key_marks = jnp.where(key_segment[:, None] == marks[None, :], masked_score, 0.0).astype(jnp.bfloat16)
    inverse_freq = rope_base ** (-2.0 * jnp.arange(HEAD // 2, dtype=jnp.float32) / HEAD)
    key_angles = inverse_freq[:, None] * key_position.astype(jnp.float32)[None, :]
    cos_keys, sin_keys = jnp.cos(key_angles), jnp.sin(key_angles)

    normed, queries, own_kv = project(tokens, attn_gain, qkv_weight, qkv_bias, cos_keys, sin_keys)
    blocks = spread_far(own_kv)
    blocks.update({o | 1: swap(blocks[o], "mp", 1) for o in sorted(blocks)})
    blocks = [blocks[o] for o in range(mp_count)]

    cot = copied(cotangent, blocks[2])
    cots = spread_far(cot)
    cots[1] = swap(cotangent, "mp", 1)
    attended, log_totals = attend(bounds, queries, query_marks, key_marks, blocks, cot)
    for o in range(2, mp_count, 2):
        cots[o | 1] = swap(cots[o], "mp", 1)

    middle, normed_mid = call(
        middle_kernel,
        [jax.ShapeDtypeStruct((tok_rows, width), jnp.float32), short(tok_rows, width)],
        [tokens, attended, out_weight, mlp_gain[None]],
        cot,
        name="middle",
    )
    gate_t, up_t = gate_weight.T, up_weight.T
    mids = {0: normed_mid, 1: swap(normed_mid, "mp", 1)}
    mids.update(spread_far(normed_mid))
    outs, grads, hids, ggs, gus = {}, {}, [], [], []
    clock = normed_mid
    for o in range(0, mp_count, 2):
        if o:
            mids[o] = after(mids[o], clock)
            mids[o | 1] = swap(mids[o], "mp", 1)
        pair = [o, o | 1]
        out, grad, hid, gg, gu = feed_forward(
            [mids[k] for k in pair], [cots[k] for k in pair], gate_t, up_t, down_weight, clock
        )
        clock = hid
        hids.append(hid), ggs.append(gg), gus.append(gu)
        for k in (0, 1):
            outs[o | k], grads[o | k] = out[k], grad[k]
    xs = [mids[o] for o in range(mp_count)]
    cs = [cots[o] for o in range(mp_count)]

    near_grads = add_pairs(grads, clock)
    clock = near_grads[0]
    dp_count = lax.axis_size("dp")
    low = bit_of("dp", 1)
    wide_down = weight_grad(cs, hids, low, 1, dp_count, clock)
    near_outs = add_pairs(outs, wide_down[0])
    wide_gate = weight_grad(xs, ggs, low, 1, dp_count, near_outs[0])
    wide_up = weight_grad(xs, gus, low, 1, dp_count, wide_gate[0])
    down_sum, gate_sum, up_sum = Scatter(wide_down), Scatter(wide_gate), Scatter(wide_up)
    clock = wide_up[0]
    near_outs = {o: after(near_outs[o], clock) if o else near_outs[o] for o in near_outs}
    outs = last_pair(near_outs, clock)
    core = bit_of("mp", 1)
    half = normed.shape[1] // 2
    grad_middle, grad_attended, *out_halves = call(
        branch_kernel,
        [jax.ShapeDtypeStruct((tok_rows, width), jnp.float32), short(q_rows, tok_rows), short(1, half, width), short(1, half, width)],
        [*last_pair(near_grads, clock), middle, mlp_gain[None], cotangent, out_weight, attended],
        clock,
        [core],
        "branch",
    )
    out_sum = Sum(*out_halves)
    clock = down_sum.step(grad_attended)
    back = functools.partial(
        attend_back,
        bounds=bounds,
        q=queries,
        query_marks=query_marks,
        key_marks=key_marks,
        o=attended,
        go=grad_attended,
        log=log_totals,
        cos_table=cos_keys,
        sin_table=sin_keys,
        blocks=blocks,
    )
    grad_qs, kv_pairs = [], []
    for head in range(KV_HEADS):
        grad_q, kv_even, kv_odd = back(head, earlier=clock)
        grad_qs.append(grad_q)
        kv_pairs += [kv_even, swap(kv_odd, "mp", 1)]
        clock = grad_q
        if head == 0:
            for item in (out_sum, gate_sum, down_sum):
                clock = item.step(clock)
            output = clock = call(output_kernel, [short(tok_rows, width)], [middle, *outs], clock, name="output")[0]
    near_kv = call(
        functools.partial(near_keys_kernel, heads=KV_HEADS),
        [short(KV_HEADS * 2 * HEAD, tok_rows)] * (mp_count // 2),
        kv_pairs,
        clock,
        name="near_keys",
    )
    kv_sums = last_pair({2 * n: a for n, a in enumerate(near_kv)}, near_kv[0])
    clock = near_kv[0]
    for item in (out_sum, up_sum, gate_sum, down_sum):
        clock = item.step(clock)
    grad_keys, grad_values = call(merge_kernel, [short(KV_HEADS * HEAD, tok_rows)] * 2, kv_sums, clock, name="merge")
    rows = [*grad_qs, grad_keys, grad_values]
    sent = outer(1 - core, normed, rows, grad_keys)
    kept = outer(core, normed, rows, sent)
    qkv_sum = Sum(sent, kept)

    clock = out_sum.step(kept)
    clock = qkv_sum.step(clock)
    grad_tokens = clock = call(
        functools.partial(tokens_kernel, count=len(rows)),
        [jax.ShapeDtypeStruct((tok_rows, width), jnp.float32)],
        [*rows, qkv_weight, tokens, attn_gain[None], grad_middle],
        clock,
        name="tokens",
        scratch=[pltpu.VMEM((qkv_weight.shape[1], tok_rows), jnp.bfloat16)],
    )[0]
    for item in (up_sum, out_sum, gate_sum, out_sum, qkv_sum, qkv_sum, out_sum, up_sum):
        clock = item.step(clock)
    for item in (down_sum, gate_sum, up_sum) * 8:
        clock = item.step(clock)
    while not out_sum.done():
        clock = out_sum.step(qkv_sum.step(clock))
    grad_out_weight, gain_line = finish(core, out_sum.kept, out_sum.came, width, clock)
    clock = gain_line
    while not qkv_sum.done():
        clock = qkv_sum.step(clock)
    grad_qkv_weight, bias_line, grad_attn_gain = finish(
        core, qkv_sum.kept, qkv_sum.came, width, clock, [qkv_weight, wide(attn_gain)[:, None]]
    )

    return (
        output,
        grad_tokens,
        grad_attn_gain[:, 0],
        grad_qkv_weight,
        bias_line[0],
        grad_out_weight,
        gain_line[0],
        gate_sum.result,
        up_sum.result,
        down_sum.result.T,
    )


def solution(mesh):
    return jax.shard_map(
        on_device,
        mesh=mesh,
        in_specs=(
            P(("dp", "mp"), None),
            P("dp", None),
            P(),
            P(),
            P(),
            P(),
            P(),
            P(None, "mp"),
            P(None, "mp"),
            P("mp", None),
            P(("dp", "mp"), None),
        ),
        out_specs=(
            P(("dp", "mp"), None),
            P(("dp", "mp"), None),
            P(),
            P(),
            P(),
            P(),
            P(),
            P("dp", "mp"),
            P("dp", "mp"),
            P("mp", "dp"),
        ),
        check_vma=False,
    )
```
